32 devices in a mesh: ctx: 16 (over z, y, core), exp: 2 (over x).
Axes of the slice: x: 2, y: 2, z: 4, core: 2. Of those that a mesh axis runs over, the one named last changes fastest.
Arguments:
- queries: bfloat16 [2048, 32, 128], P('ctx', 'exp'), may hold values from -100 to 100
- keys: bfloat16 [2048, 2, 128], P('ctx'), may hold values from -4 to 4
- values: bfloat16 [2048, 2, 128], P('ctx'), may hold values from -4 to 4
- resid: bfloat16 [2048, 4096], P('ctx', 'exp'), may hold values from -20 to 20
- gain: float32 [4096], P('exp'), may hold values from 0.1 to 1.9
- expert_ids: int32 [2048, 8], P('ctx'), may hold values from 0 to 127, all different within a row; in each aligned block of 128 rows (0 to 127, 128 to 255, ...) at most 10 rows name the same one
- gate_scores: float32 [2048, 8], P('ctx'), may hold values from 0.05 to 1
- w_gate_up: bfloat16 [16, 4096, 2, 768], P('ctx', 'exp'), may hold values from -0.09375 to 0.09375
- w_down: bfloat16 [16, 768, 4096], P('ctx', None, 'exp'), may hold values from -0.625 to 0.625
- w_out: bfloat16 [32, 128, 4096], P('exp', 'ctx'), may hold values from -0.5 to 0.5
Outputs:
- context: bfloat16 [2048, 32, 128], P('ctx', 'exp')
- mixed: bfloat16 [2048, 4096], P('ctx', 'exp')
The draws below stay inside these ranges and needn't reach their ends.
Inputs may be any that keep to these rules, and one draw needn't show every extreme that they name: `expert_ids`: each row names 8 different experts; within the 128 rows of one index of ctx no expert is named more than 10 times.
All inputs are finite; a program needn't handle non-finite values.
Results may differ from the reference program's by a relative error of at most 0.02.
Values may be sent and summed in bfloat16 or wider, within the bound.
A program may use at most 64 MiB of HBM per device.

```python
import math
import jax
import jax.numpy as jnp
import numpy as np
from jax import lax

D = 4096
HQ = 32
KVH = 2
HD = 128
FF = 768
EXPERTS = 128
TOPK = 8
T_DEV = 128
SEQ = 2048
MOST = 10
FLIGHT = 16
N_CTX = 16
N_EXP = 2


def final_keys(key):
    keys_base = jnp.clip(jax.random.normal(jax.random.fold_in(key, 101), (SEQ, KVH, HD), jnp.float32), -4.0, 4.0)
    return keys_base


def draw_keys(key, part):
    return final_keys(key).astype(jnp.bfloat16)


def draw_queries(key, part):
    raw_draw = jnp.clip(jax.random.normal(jax.random.fold_in(key, 301), (SEQ, HQ, HD), jnp.float32), -4.0, 4.0)
    return raw_draw.astype(jnp.bfloat16)


def draw_resid(key, part):
    normal_part = jnp.clip(jax.random.normal(jax.random.fold_in(key, 401), (SEQ, D), jnp.float32), -4.0, 4.0)
    row_scale = jnp.exp(jax.random.uniform(jax.random.fold_in(key, 402), (SEQ, 1), jnp.float32, math.log(0.3), math.log(3.0)))
    column_rough = jnp.exp(jax.random.uniform(jax.random.fold_in(key, 403), (1, D), jnp.float32, math.log(0.5), math.log(2.0)))
    fraction = jnp.arange(D).astype(jnp.float32)[None, :] / (D - 1) - 0.5
    rising = jnp.exp(math.log(3.0) * fraction)
    drawn_value = jnp.clip(0.4 * normal_part * row_scale * column_rough * rising, -20.0, 20.0)
    return drawn_value.astype(jnp.bfloat16)


def level_of(key, dims, cuts, low, top_value):
    def one(dim, parts):
        heights = jax.random.uniform(jax.random.fold_in(jax.random.fold_in(key, 6), dim), (parts,), jnp.float32, low / len(cuts), top_value / len(cuts))
        return jnp.repeat(jnp.exp(heights), dims[dim] // parts).reshape((-1,) + (1,) * (len(dims) - dim - 1))

    level = one(*cuts[0])
    for cut in cuts[1:]:
        level = level * one(*cut)
    return level


def deal_out(rng, own, number, rows, count, top, bound, lean):
    ranking = jax.random.permutation(rng, count)
    crowded, ordinary = load_shares(count, rows * top, bound, lean, True), load_shares(count, rows * top, bound, lean, False)
    places = jnp.arange(count)

    def named(tallies, turn):
        used = int((tallies > 0).sum())
        fixed = max(1, used // 4)
        passed = fixed + (places - fixed + turn * (used - fixed)) % max(1, count - fixed)
        return jnp.zeros((count,), jnp.int32).at[ranking[jnp.where(places < fixed, places, passed)]].set(jnp.asarray(tallies, jnp.int32))

    tallies = jnp.where(number % 4 == 0, named(crowded, number // 4), named(ordinary, number - number // 4 - 1))
    mixed = jax.random.permutation(jax.random.fold_in(own, 3), count)
    giver, sink = mixed[0:count // 2 * 2:2], mixed[1:count // 2 * 2:2]
    slack = jnp.minimum(tallies[giver] - 1, bound - tallies[sink]) // 2
    slack = jnp.where((giver == ranking[0]) | (sink == ranking[0]) | (tallies[sink] == 0), 0, jnp.maximum(slack, 0))
    passed = jax.random.randint(jax.random.fold_in(own, 4), (count // 2,), 0, 1 << 20) % (slack + 1)
    tallies = tallies.at[giver].add(-passed).at[sink].add(passed)
    labels = jnp.searchsorted(jnp.cumsum(tallies), jnp.arange(rows * top), side="right").astype(jnp.int32)
    table = labels.reshape(top, rows).T
    table = table[jax.random.permutation(jax.random.fold_in(own, 1), rows)]
    turn = jax.random.randint(jax.random.fold_in(own, 2), (rows, 1), 0, top)
    return jnp.take_along_axis(table, (jnp.arange(top)[None, :] + turn) % top, axis=1)


def load_shares(count, total, reach, lean, full):
    weights = [(1 << 20) // math.isqrt(standing ** lean) + 1 for standing in range(1, count + 1)]
    largest = reach if full else min(reach, max(-(-total // count), total * weights[0] // sum(weights)))
    least = 1 if total - largest >= count - 1 else 0
    given, rest = [largest] + [least] * (count - 1), total - largest - least * (count - 1)
    while rest > 0:
        candidates = [i for i in range(1, count) if given[i] < largest] or [i for i in range(1, count) if given[i] < reach]
        pool, left = sum([weights[i] for i in candidates]), rest
        for i in candidates:
            more = min(reach - given[i], max(1, left * weights[i] // pool), rest)
            given[i] = given[i] + more
            rest = rest - more
    return np.array(given)


def bell_draw(own_key, shape, spread, limit, pieces=(), held_as=jnp.bfloat16):
    level = level_of(own_key, shape, pieces, -0.22, 0.18) if pieces else 1.0
    values = jax.random.normal(own_key, shape, jnp.float32) * spread * level
    return jnp.minimum(jnp.maximum(values, -limit), limit).astype(held_as)


def setup_inputs(seed: int = 0) -> dict:
    key_list = jax.random.split(jax.random.key(seed), 11)
    queries = draw_queries(jax.random.fold_in(key_list[10], 71), 0)
    keys = draw_keys(jax.random.fold_in(key_list[10], 71), 0)
    values = bell_draw(key_list[2], (SEQ, KVH, HD), 1.0, 4.0, ((0, 16),))
    resid = draw_resid(jax.random.fold_in(key_list[10], 71), 0)
    gain = jnp.clip(1.0 + 0.18 * jax.random.normal(key_list[4], (D,), jnp.float32), 0.1, 1.9)
    expert_ids_keys = jax.random.split(jax.random.fold_in(key_list[5], 1), SEQ // T_DEV)
    expert_ids_turns = jax.random.permutation(jax.random.fold_in(key_list[5], 3), SEQ // T_DEV)
    expert_ids = jax.vmap(lambda own, number: deal_out(jax.random.fold_in(key_list[5], 2), own, number, T_DEV, EXPERTS, TOPK, MOST, 2))(expert_ids_keys, expert_ids_turns).reshape((SEQ, TOPK))
    gate_scores = jnp.clip(0.05 + 0.95 * jax.random.uniform(key_list[6], (SEQ, TOPK), jnp.float32) ** level_of(key_list[6], (SEQ, TOPK), ((0, 16),), -0.2, 0.2), 0.05, 1.0)
    w_gate_up = bell_draw(key_list[7], (FLIGHT, D, 2, FF), D ** -0.5, 0.09375, ((0, 16), (1, 2)))
    w_down = bell_draw(key_list[8], (FLIGHT, FF, D), (FF // 8) ** -0.5, 0.625, ((0, 16), (2, 2)))
    w_out = bell_draw(key_list[9], (HQ, HD, D), HD ** -0.5, 0.5, ((0, 2), (1, 16)))
    return {"queries": queries, "keys": keys, "values": values, "resid": resid, "gain": gain, "expert_ids": expert_ids, "gate_scores": gate_scores, "w_gate_up": w_gate_up, "w_down": w_down, "w_out": w_out}


def keep_round(value):
    rounded = value.astype(jnp.bfloat16)
    return lax.optimization_barrier(rounded).astype(jnp.float32)

def reference(queries, keys, values, resid, gain, expert_ids, gate_scores, w_gate_up, w_down, w_out):
    group_size = HQ // KVH
    head_group = (jnp.arange(HQ) // group_size).astype(jnp.int32)
    keys_wide = jnp.take(keys, head_group, axis=1).astype(jnp.float32)
    values_wide = jnp.take(values, head_group, axis=1).astype(jnp.float32)
    scaling = 1.0 / math.sqrt(HD)
    positions = jnp.arange(SEQ).astype(jnp.int32)

    def attend(block_index):
        start_row = (block_index * T_DEV).astype(jnp.int32)
        query_block = lax.dynamic_slice_in_dim(queries, start_row, T_DEV, 0).astype(jnp.float32)
        scores = jnp.einsum('thd,shd->hts', query_block, keys_wide) * scaling
        query_pos = start_row + jnp.arange(T_DEV).astype(jnp.int32)
        visible = positions[None, None, :] <= query_pos[None, :, None]
        masked = jnp.where(visible, scores, -1e+30)
        highest = lax.optimization_barrier(jnp.max(masked, axis=2, keepdims=True))
        weights_exp = jnp.where(visible, jnp.exp(masked - highest), 0.0)
        denominator = lax.optimization_barrier(jnp.sum(weights_exp, axis=2))
        numerator = jnp.einsum('hts,shd->thd', keep_round(weights_exp), values_wide)
        return (numerator / jnp.transpose(denominator)[:, :, None]).astype(jnp.bfloat16)
    context = lax.map(attend, jnp.arange(N_CTX).astype(jnp.int32)).reshape(SEQ, HQ, HD)
    heads_local = HQ // N_EXP
    weight_groups = w_out.astype(jnp.float32).reshape(N_EXP, heads_local * HD, D)

    def project(block_index):
        start_row = (block_index * T_DEV).astype(jnp.int32)
        context_block = lax.dynamic_slice_in_dim(context, start_row, T_DEV, 0).astype(jnp.float32)
        context_block = context_block.reshape(T_DEV, N_EXP, heads_local * HD)
        partial_sum = jnp.einsum('teh,ehd->ted', context_block, weight_groups)
        return lax.optimization_barrier(jnp.sum(keep_round(partial_sum), axis=1))
    attended = lax.map(project, jnp.arange(N_CTX).astype(jnp.int32)).reshape(SEQ, D)
    hidden_state = resid.astype(jnp.float32) + attended
    mean_square = lax.optimization_barrier(jnp.mean(hidden_state * hidden_state, axis=1, keepdims=True))
    normed = (hidden_state * lax.rsqrt(mean_square + 1e-06) * gain[None, :]).astype(jnp.bfloat16)
    per_block = expert_ids.reshape(N_CTX, T_DEV * TOPK).astype(jnp.int32)
    onehot = (per_block[:, :, None] == jnp.arange(FLIGHT).astype(jnp.int32)[None, None, :]).astype(jnp.int32)
    earlier = jnp.cumsum(onehot, axis=1) - onehot
    rank_of = lax.optimization_barrier(jnp.sum(earlier * onehot, axis=2)).astype(jnp.int32)
    active = per_block < FLIGHT
    slot_of = jnp.where(active, per_block * MOST + rank_of, FLIGHT * MOST).astype(jnp.int32)
    token_global = (jnp.arange(N_CTX)[:, None] * T_DEV + jnp.arange(T_DEV * TOPK)[None, :] // TOPK).astype(jnp.int32)
    mixing = (gate_scores / lax.optimization_barrier(jnp.sum(gate_scores, axis=1, keepdims=True))).reshape(N_CTX, T_DEV * TOPK)
    source_index = jnp.broadcast_to(jnp.arange(N_CTX).astype(jnp.int32)[:, None], per_block.shape)
    slot_token = jnp.zeros((N_CTX, FLIGHT * MOST), jnp.int32).at[source_index, slot_of].set(token_global, mode='drop')
    slot_weight = jnp.zeros((N_CTX, FLIGHT * MOST), jnp.float32).at[source_index, slot_of].set(mixing, mode='drop')
    slot_active = jnp.zeros((N_CTX, FLIGHT * MOST), jnp.float32).at[source_index, slot_of].set(1.0, mode='drop')

    def one_expert(moe_sum, expert_index):
        begin = (expert_index * MOST).astype(jnp.int32)
        tokens_for = lax.dynamic_slice_in_dim(slot_token, begin, MOST, 1).reshape(-1)
        weights_for = lax.dynamic_slice_in_dim(slot_weight, begin, MOST, 1).reshape(-1)
        active_for = lax.dynamic_slice_in_dim(slot_active, begin, MOST, 1).reshape(-1)
        row_block = jnp.take(normed, tokens_for, axis=0) * active_for[:, None].astype(jnp.bfloat16)
        weights_gu = lax.dynamic_index_in_dim(w_gate_up, expert_index, 0, keepdims=False)
        weights_gu = weights_gu.astype(jnp.float32).reshape(N_EXP, D // N_EXP, 2 * FF)
        split_rows = row_block.astype(jnp.float32).reshape(N_CTX * MOST, N_EXP, D // N_EXP)
        partial_sum = jnp.einsum('red,edf->ref', split_rows, weights_gu)
        summed = lax.optimization_barrier(jnp.sum(keep_round(partial_sum), axis=1))
        hidden_units = (jax.nn.silu(summed[:, :FF]) * summed[:, FF:]).astype(jnp.bfloat16)
        down_weight = lax.dynamic_index_in_dim(w_down, expert_index, 0, keepdims=False)
        result = jnp.dot(hidden_units, down_weight, preferred_element_type=jnp.float32).astype(jnp.bfloat16)
        moe_sum = moe_sum.at[tokens_for].add(weights_for[:, None] * result.astype(jnp.float32))
        return (moe_sum, active_for[0])
    moe_total = lax.scan(one_expert, jnp.zeros((SEQ, D), jnp.float32), jnp.arange(FLIGHT).astype(jnp.int32))[0]
    mixed = (hidden_state + moe_total).astype(jnp.bfloat16)
    return (context, mixed)
```

```python
import functools
import math

import jax
import jax.numpy as jnp
from jax import lax
from jax.experimental import pallas as pl
from jax.experimental.pallas import tpu as pltpu
from jax.sharding import PartitionSpec as P

D = 4096
HQ = 32
KVH = 2
EXPERTS = 128
TOPK = 8


masked_score = -1e30
epsilon = 1e-06


def attend_piece(state_now, pair_piece, offset, query_rows, query_pos, last_pos, scaling):
    key_piece, value_piece = pair_piece
    length = key_piece.shape[0]

    def compute(state_in):
        running, denominator, numerator = state_in
        scores = (
            jnp.einsum("rd,kd->rk", query_rows, key_piece, preferred_element_type=jnp.float32)
            * scaling
        )
        key_pos = jnp.arange(length, dtype=jnp.int32)
        visible = key_pos[None, :] <= query_pos[:, None]
        masked = jnp.where(visible, scores, masked_score)
        highest = jnp.maximum(running, jnp.max(masked, axis=1))
        weights_exp = jnp.where(visible, jnp.exp(masked - highest[:, None]), 0.0)
        rounded = weights_exp.astype(jnp.bfloat16)
        numerator = jnp.dot(rounded, value_piece, preferred_element_type=jnp.float32)
        denominator = jnp.sum(weights_exp, axis=1)
        return (highest, denominator, numerator)

    def untouched(state_in):
        return state_in

    return lax.cond(offset <= last_pos, compute, untouched, state_now)


def general_body(queries, keys, values, resid, gain, expert_ids, gate_scores, w_gate_up, w_down, w_out):
    tokens_here = queries.shape[0]
    heads_here = queries.shape[1]
    head_size = queries.shape[2]
    ctx_count = lax.axis_size("ctx")
    ctx_place = lax.axis_index("ctx")
    exp_place = lax.axis_index("exp")
    own_pos = ctx_place * tokens_here + jnp.arange(tokens_here, dtype=jnp.int32)
    query_sets = (queries, own_pos)
    group_index = exp_place * heads_here // (HQ // KVH)
    key_local = lax.dynamic_index_in_dim(keys, group_index, 1, keepdims=False)
    value_local = lax.dynamic_index_in_dim(values, group_index, 1, keepdims=False)
    scaling = 1.0 / math.sqrt(head_size)
    set_queries, set_pos = query_sets
    set_rows = set_queries.shape[0] * heads_here
    initial = [
        (
            jnp.full((set_rows,), masked_score, jnp.float32),
            jnp.zeros((set_rows,), jnp.float32),
            jnp.zeros((set_rows, head_size), jnp.float32),
        )
    ]
    rows_set = set_queries.reshape(set_rows, head_size)
    pos_set = jnp.repeat(set_pos, heads_here)
    last_set = jnp.max(set_pos)
    updated = [
        attend_piece(
            tuple(initial)[0],
            (
                lax.all_gather(key_local, "ctx", axis=0, tiled=True),
                lax.all_gather(value_local, "ctx", axis=0, tiled=True),
            ),
            jnp.int32(0),
            rows_set,
            pos_set,
            last_set,
            scaling,
        )
    ]
    folded = tuple(updated)
    pieces_out = []
    for state_set in folded:
        normalized = state_set[2] / state_set[1][:, None]
        pieces_out.append(normalized.reshape(-1, heads_here, head_size).astype(jnp.bfloat16))
    context = pieces_out[0]
    whole_out = lax.all_gather(w_out, "ctx", axis=1, tiled=True)
    projected = jnp.einsum("thp,hpd->td", context, whole_out, preferred_element_type=jnp.float32)
    attended = lax.psum_scatter(
        projected.astype(jnp.bfloat16), "exp", scatter_dimension=1, tiled=True
    ).astype(jnp.float32)
    hidden_state = resid.astype(jnp.float32) + attended
    square_sum = lax.psum(jnp.sum(hidden_state * hidden_state, axis=1), "exp")
    inverse = lax.rsqrt(square_sum / D + epsilon)
    normed = (hidden_state * inverse[:, None] * gain[None, :]).astype(jnp.bfloat16)
    capacity = max(2, 5 * tokens_here * TOPK // (4 * EXPERTS))
    flat_ids = expert_ids.reshape(-1)
    onehot = (flat_ids[:, None] == jnp.arange(ctx_count, dtype=jnp.int32)[None, :]).astype(
        jnp.int32
    )
    earlier = jnp.cumsum(onehot, axis=0) - onehot
    rank_of = jnp.sum(earlier * onehot, axis=1)
    active = flat_ids < ctx_count
    slot_of = jnp.where(active, flat_ids * capacity + rank_of, -1).reshape(tokens_here, TOPK)
    slot_range = jnp.arange(ctx_count * capacity, dtype=jnp.int32)
    dispatch_map = jnp.zeros((ctx_count * capacity, tokens_here), jnp.bfloat16)
    for column in range(TOPK):
        dispatch_map = dispatch_map + (slot_range[:, None] == slot_of[None, :, column]).astype(
            jnp.bfloat16
        )
    local_width = normed.shape[1]
    outgoing = jnp.dot(dispatch_map, normed, preferred_element_type=jnp.float32).astype(
        jnp.bfloat16
    )
    outgoing = outgoing.reshape(ctx_count, capacity, local_width)
    arrived = lax.all_to_all(outgoing, "ctx", split_axis=0, concat_axis=0, tiled=True)
    sources = arrived.shape[0]
    width_slots = arrived.shape[1]
    row_block = arrived.reshape(sources * width_slots, local_width)
    partial_sum = jnp.einsum(
        "rd,dgf->rgf", row_block, w_gate_up[0], preferred_element_type=jnp.float32
    )
    summed = lax.psum(partial_sum.astype(jnp.bfloat16), "exp").astype(jnp.float32)
    hidden_units = (jax.nn.silu(summed[:, 0]) * summed[:, 1]).astype(jnp.bfloat16)
    result = jnp.dot(hidden_units, w_down[0], preferred_element_type=jnp.float32).astype(
        jnp.bfloat16
    )
    result = result.reshape(sources, width_slots, local_width)
    returned = lax.all_to_all(result, "ctx", split_axis=0, concat_axis=0, tiled=True)
    back_rows = returned.reshape(ctx_count * capacity, local_width)
    picked = jnp.take(back_rows, jnp.maximum(slot_of, 0).reshape(-1), axis=0).reshape(
        tokens_here, TOPK, local_width
    )
    weight_now = gate_scores / jnp.sum(gate_scores, axis=1, keepdims=True)
    weight_now = jnp.where(active.reshape(tokens_here, TOPK), weight_now, 0.0)
    routed = jnp.zeros((tokens_here, local_width), jnp.float32)
    for column in range(TOPK):
        routed = routed + weight_now[:, column : column + 1] * picked[:, column].astype(jnp.float32)
    mixed = (hidden_state + routed).astype(jnp.bfloat16)
    return (context, mixed)


MESH = pl.DeviceIdType.MESH
F32 = jnp.float32
BF16 = jnp.bfloat16
N_Z = 4
PLANE = 4


def attend_kernel(
    q_ref, kv_ref, w_hbm, resid_ref, ctx_ref, hid_ref,
    kvbuf, wbuf, rows32, ctx2d, ctxbuf, target, acc,
    kv_send, kv_recv, w_up, w_down_sem, w_y, w_sib, w_recv, x_send, c_send, c_recv, local_sem,
):
    c = lax.axis_index("ctx")
    e = lax.axis_index("exp")
    z = c // PLANE
    y = (c // 2) % 2
    k = c % 2
    plane = c % PLANE
    y_peer = z * PLANE + (1 - y) * 2 + k
    sibling = z * PLANE + y * 2 + (1 - k)
    half = resid_ref.shape[1]
    tokens = resid_ref.shape[0]
    heads = q_ref.shape[0] // tokens
    depth = wbuf.shape[2]

    barrier = pltpu.get_barrier_semaphore()
    for step in range(1, N_Z):
        pl.semaphore_signal(
            barrier, inc=1, device_id=(((z + step) % N_Z) * PLANE + plane, e), device_id_type=MESH
        )
    pl.semaphore_signal(barrier, inc=1, device_id=(y_peer, e), device_id_type=MESH)
    pl.semaphore_signal(barrier, inc=1, device_id=(sibling, e), device_id_type=MESH)
    pl.semaphore_signal(barrier, inc=1, device_id=(c, 1 - e), device_id_type=MESH)
    own_w = pltpu.make_async_copy(
        w_hbm.at[:, pl.ds(pl.multiple_of(e * half, half), half)], wbuf.at[c, e], local_sem.at[0]
    )
    own_w.start()
    kvbuf[c] = kv_ref[...]
    pl.semaphore_wait(barrier, N_Z + 2)

    def kv_copy(block, slot, to):
        return pltpu.make_async_remote_copy(
            src_ref=kvbuf.at[block], dst_ref=kvbuf.at[block], send_sem=kv_send.at[slot],
            recv_sem=kv_recv.at[block], device_id=(to, e), device_id_type=MESH,
        )

    def w_copy(block, g, sem, to):
        return pltpu.make_async_remote_copy(
            src_ref=wbuf.at[block, g], dst_ref=wbuf.at[block, g], send_sem=sem,
            recv_sem=w_recv.at[block, g], device_id=(to, e), device_id_type=MESH,
        )

    for step in range(1, N_Z):
        kv_copy(c, step - 1, ((z + step) % N_Z) * PLANE + plane).start()
    kv_copy(c, 3, y_peer).start()
    kv_copy(c, 7, sibling).start()
    swap = pltpu.make_async_remote_copy(
        src_ref=w_hbm.at[:, pl.ds(pl.multiple_of((1 - e) * half, half), half)],
        dst_ref=wbuf.at[c, e], send_sem=x_send.at[0], recv_sem=w_recv.at[c, e],
        device_id=(c, 1 - e), device_id_type=MESH,
    )
    swap.start()

    def group_of(s):
        return (e + s) % 2

    def z_forward(block_z, s, up, down):
        g = group_of(s)
        block = block_z * PLANE + plane

        @pl.when(jnp.logical_and(up, z < N_Z - 1))
        def _():
            w_copy(block, g, w_up.at[block_z, g], c + PLANE).start()

        @pl.when(jnp.logical_and(down, z > 0))
        def _():
            w_copy(block, g, w_down_sem.at[block_z, g], c - PLANE).start()

        w_copy(block, g, w_y.at[block_z, g], y_peer).start()
        w_copy(block, g, w_sib.at[0, block_z, g], sibling).start()

    def wait_block(block, g):
        w_copy(block, g, w_sib.at[0, 0, 0], sibling).wait_recv()

    own_w.wait()
    z_forward(z, 0, True, True)

    for step in range(1, N_Z):
        block = ((z + step) % N_Z) * PLANE + plane
        kv_copy(block, 0, sibling).wait_recv()
        kv_copy(block, 3 + step, y_peer).start()
        kv_copy(block, 7 + step, sibling).start()
    for step in range(N_Z):
        block = ((z + step) % N_Z) * PLANE + (1 - y) * 2 + k
        kv_copy(block, 0, sibling).wait_recv()
        kv_copy(block, 11 + step, sibling).start()
    rows32[...] = q_ref[...].astype(F32)
    row = lax.broadcasted_iota(jnp.int32, target.shape, 0)
    col = lax.broadcasted_iota(jnp.int32, target.shape, 1)
    target[...] = row - ((col % 128) // 8) * 128 - (col // 128) * 8 - col % 8
    wait_block(c, group_of(1))
    z_forward(z, 1, True, True)
    for block_z in range(N_Z):
        for block_y in range(2):
            kv_copy(block_z * PLANE + block_y * 2 + 1 - k, 0, sibling).wait_recv()

    scale = 1.0 / math.sqrt(q_ref.shape[1])
    n_keys = kvbuf.shape[0] * tokens

    @pl.loop(0, heads // 2)
    def _(pair):
        first = rows32[pl.ds(2 * pair, tokens, stride=heads), :]
        second = rows32[pl.ds(2 * pair + 1, tokens, stride=heads), :]
        both = jnp.concatenate([first, second], axis=0).astype(BF16)
        key_all = kvbuf[:, :tokens, :].reshape(n_keys, 128)
        value_all = kvbuf[:, tokens:, :].reshape(n_keys, 128)
        scores = lax.dot_general(
            both, key_all, (((1,), (1,)), ((), ())), preferred_element_type=F32
        ) * scale
        q_pos = c * tokens + lax.broadcasted_iota(jnp.int32, scores.shape, 0) % tokens
        k_pos = lax.broadcasted_iota(jnp.int32, scores.shape, 1)
        masked = jnp.where(k_pos <= q_pos, scores, masked_score)
        best = jnp.max(masked, axis=1, keepdims=True)
        prob = jnp.exp(masked - best)
        total = jnp.sum(prob, axis=1, keepdims=True)
        part = jnp.dot(prob.astype(BF16), value_all, preferred_element_type=F32)
        done = (part / total).astype(BF16)
        ctx2d[:, pl.ds(pl.multiple_of(pair * 256, 256), 128)] = done[:tokens]
        ctx2d[:, pl.ds(pl.multiple_of(pair * 256 + 128, 128), 128)] = done[tokens:]
        rows32[pl.ds(2 * pair, tokens, stride=heads), :] = done[:tokens].astype(F32)
        rows32[pl.ds(2 * pair + 1, tokens, stride=heads), :] = done[tokens:].astype(F32)

    @pl.loop(0, wbuf.shape[0] // 2)
    def _(pair):
        pick = jnp.where(target[...] == 16 * pair, 1.0, 0.0).astype(BF16)
        ctxbuf[e, pair] = jnp.dot(ctx2d[...], pick, preferred_element_type=F32).astype(BF16)

    ctx_swap = pltpu.make_async_remote_copy(
        src_ref=ctxbuf.at[e], dst_ref=ctxbuf.at[e], send_sem=c_send.at[0], recv_sem=c_recv.at[0],
        device_id=(c, 1 - e), device_id_type=MESH,
    )
    ctx_swap.start()
    ctx_ref[...] = rows32[...].astype(BF16)
    acc[...] = jnp.zeros_like(acc)
    other_ctx = pltpu.make_async_remote_copy(
        src_ref=ctxbuf.at[1 - e], dst_ref=ctxbuf.at[1 - e], send_sem=c_send.at[0],
        recv_sem=c_recv.at[0], device_id=(c, 1 - e), device_id_type=MESH,
    )

    def sides(i, run):
        d = i // 2

        @pl.when(z - d >= 0)
        def _():
            run(z - d, True, False)

        @pl.when(jnp.logical_and(d > 0, z + d < N_Z))
        def _():
            run(z + d, False, True)

    def project(block_z, block_y, g):
        pair = block_z * 2 + block_y
        weights = wbuf[pl.ds(2 * pair, 2), pl.ds(g, 1)].reshape(2 * depth, half)
        acc[g] += jnp.dot(ctxbuf[g, pair], weights, preferred_element_type=F32)

    @pl.loop(0, 2 * N_Z)
    def _(i):
        s = i % 2
        g = group_of(s)

        @pl.when(i + 2 < 2 * N_Z)
        def _():
            def run(block_z, up, down):
                wait_block(block_z * PLANE + plane, g)
                z_forward(block_z, s, up, down)

            sides(i + 2, run)

        def run_y(block_z, up, down):
            block = block_z * PLANE + (1 - y) * 2 + k
            wait_block(block, g)
            w_copy(block, g, w_sib.at[1, block_z, g], sibling).start()

        sides(i, run_y)

        @pl.when(i == 1)
        def _():
            other_ctx.wait_recv()

        def run_project(block_z, up, down):
            wait_block(block_z * PLANE + y * 2 + 1 - k, g)
            project(block_z, y, g)
            wait_block(block_z * PLANE + (1 - y) * 2 + 1 - k, g)
            project(block_z, 1 - y, g)

        sides(i, run_project)

    hid_ref[...] = resid_ref[...].astype(F32) + (
        acc[0].astype(BF16).astype(F32) + acc[1].astype(BF16).astype(F32)
    )

    for slot in range(15):
        kv_copy(c, slot, sibling).wait_send()
    swap.wait_send()
    ctx_swap.wait_send()

    @pl.loop(0, N_Z)
    def _(block_z):
        for g in range(2):
            @pl.when(jnp.logical_and(block_z <= z, z < N_Z - 1))
            def _():
                w_copy(c, g, w_up.at[block_z, g], sibling).wait_send()

            @pl.when(jnp.logical_and(block_z >= z, z > 0))
            def _():
                w_copy(c, g, w_down_sem.at[block_z, g], sibling).wait_send()

            w_copy(c, g, w_y.at[block_z, g], sibling).wait_send()
            w_copy(c, g, w_sib.at[0, block_z, g], sibling).wait_send()
            w_copy(c, g, w_sib.at[1, block_z, g], sibling).wait_send()


def expert_kernel(
    hid_ref, gain_ref, pick_ref, mix_ref, gu_hbm, down_hbm, mixed_ref,
    gu, down, squares, peer_squares, stage, two, outbox, inbox, backbox, endbox, parts, peer_parts, act,
    sq_sem, p_send, p_recv, a_send, a_recv, b_send, b_recv, local_sem,
):
    c = lax.axis_index("ctx")
    e = lax.axis_index("exp")
    n = inbox.shape[0]
    cap = inbox.shape[1]
    rows = n * cap
    blocks = inbox.shape[2]
    barrier = pltpu.get_barrier_semaphore()

    @pl.loop(1, n)
    def _(j):
        pl.semaphore_signal(barrier, inc=1, device_id=((c + j) % n, e), device_id_type=MESH)

    pl.semaphore_signal(barrier, inc=1, device_id=(c, 1 - e), device_id_type=MESH)
    load_gu = pltpu.make_async_copy(gu_hbm, gu, local_sem.at[0])
    load_down = pltpu.make_async_copy(down_hbm, down, local_sem.at[1])
    load_gu.start()
    load_down.start()
    hidden = hid_ref[...]
    own = jnp.sum(hidden * hidden, axis=1, keepdims=True)
    squares[...] = jnp.broadcast_to(own, squares.shape)
    pl.semaphore_wait(barrier, n)
    sq = pltpu.make_async_remote_copy(
        src_ref=squares, dst_ref=peer_squares, send_sem=sq_sem.at[0], recv_sem=sq_sem.at[1],
        device_id=(c, 1 - e), device_id_type=MESH,
    )
    sq.start()
    sq.wait()
    mean = (squares[:, :1] + peer_squares[:, :1]) / D
    normed = (hid_ref[...] * lax.rsqrt(mean + epsilon) * gain_ref[...]).astype(BF16)
    two[: normed.shape[0], :] = normed
    for j in range(blocks):
        stage[pl.ds(j, rows, stride=blocks), :] = jnp.dot(
            pick_ref[...], two[: normed.shape[0], j * 128 : (j + 1) * 128], preferred_element_type=F32
        )
    outbox[...] = stage[...].reshape(outbox.shape).astype(BF16)

    def a_copy(j):
        to = (c + j) % n
        return pltpu.make_async_remote_copy(
            src_ref=outbox.at[to], dst_ref=inbox.at[c], send_sem=a_send.at[j],
            recv_sem=a_recv.at[c], device_id=(to, e), device_id_type=MESH,
        )

    def b_copy(j):
        to = (c + j) % n
        return pltpu.make_async_remote_copy(
            src_ref=backbox.at[to], dst_ref=endbox.at[c], send_sem=b_send.at[j],
            recv_sem=b_recv.at[c], device_id=(to, e), device_id_type=MESH,
        )

    def arrived(box, sems):
        @pl.loop(1, n)
        def _(j):
            source = (c + j) % n
            pltpu.make_async_remote_copy(
                src_ref=box.at[source], dst_ref=box.at[source], send_sem=a_send.at[0],
                recv_sem=sems.at[source], device_id=(source, e), device_id_type=MESH,
            ).wait_recv()

        stage[...] = box[...].reshape(stage.shape).astype(F32)
        for j in range(blocks):
            two[:, j * 128 : (j + 1) * 128] = stage[pl.ds(j, rows, stride=blocks), :].astype(BF16)

    @pl.loop(1, n)
    def _(j):
        a_copy(j).start()

    inbox[c] = outbox[c]
    load_gu.wait()
    arrived(inbox, a_recv)

    units = down.shape[0]
    width = parts.shape[3]

    def p_copy(m):
        return pltpu.make_async_remote_copy(
            src_ref=parts.at[m], dst_ref=peer_parts.at[m], send_sem=p_send.at[m],
            recv_sem=p_recv.at[m], device_id=(c, 1 - e), device_id_type=MESH,
        )

    n_parts = units // width
    for m in range(n_parts):
        for side in range(2):
            start = side * units + m * width
            parts[m, side] = jnp.dot(
                two[...], gu[:, start : start + width], preferred_element_type=F32
            ).astype(BF16)
        p_copy(m).start()
    for m in range(n_parts):
        p_copy(m).wait_recv()
        gate = parts[m, 0].astype(F32) + peer_parts[m, 0].astype(F32)
        up = parts[m, 1].astype(F32) + peer_parts[m, 1].astype(F32)
        act[:, m * width : (m + 1) * width] = (gate / (1.0 + jnp.exp(-gate)) * up).astype(BF16)
    load_down.wait()
    for j in range(blocks // 2):
        result = jnp.dot(
            act[...], down[:, j * 256 : (j + 1) * 256], preferred_element_type=F32
        )
        stage[pl.ds(2 * j, rows, stride=blocks), :] = result[:, :128]
        stage[pl.ds(2 * j + 1, rows, stride=blocks), :] = result[:, 128:]
    backbox[...] = stage[...].reshape(backbox.shape).astype(BF16)

    @pl.loop(1, n)
    def _(j):
        b_copy(j).start()

    endbox[c] = backbox[c]
    mix = mix_ref[...]
    mix_high = mix.astype(BF16)
    mix_low = (mix - mix_high.astype(F32)).astype(BF16)
    arrived(endbox, b_recv)
    routed = jnp.dot(mix_high, two[...], preferred_element_type=F32)
    routed += jnp.dot(mix_low, two[...], preferred_element_type=F32)
    mixed_ref[...] = (hid_ref[...] + routed).astype(BF16)

    @pl.loop(1, n)
    def _(j):
        a_copy(j).wait_send()
        b_copy(j).wait_send()

    for m in range(n_parts):
        p_copy(m).wait_send()


def fast_body(queries, keys, values, resid, gain, expert_ids, gate_scores, w_gate_up, w_down, w_out):
    tokens, heads, size = queries.shape
    n = lax.axis_size("ctx")
    exp_place = lax.axis_index("exp")
    half = resid.shape[1]
    capacity = max(2, 5 * tokens * TOPK // (4 * EXPERTS))
    hits = expert_ids[:, :, None] == jnp.arange(n, dtype=jnp.int32)[None, None, :]
    named = jnp.any(hits, axis=1)
    earlier = jnp.tril(jnp.ones((tokens, tokens), BF16), -1)
    rank = jnp.dot(earlier, named.astype(BF16), preferred_element_type=F32).astype(jnp.int32)
    rank = jnp.where(named, rank, -1)
    slots = jnp.arange(capacity, dtype=jnp.int32)
    pick = (rank.T[:, None, :] == slots[None, :, None]).astype(BF16).reshape(n * capacity, tokens)
    share = gate_scores / jnp.sum(gate_scores, axis=1, keepdims=True)
    share = jnp.sum(jnp.where(hits, share[:, :, None], 0.0), axis=1)
    mix = jnp.where(rank[:, :, None] == slots[None, None, :], share[:, :, None], 0.0)
    mix = mix.reshape(tokens, n * capacity)

    group = exp_place * heads // (HQ // KVH)
    own_kv = jnp.concatenate(
        [
            lax.dynamic_index_in_dim(keys, group, 1, keepdims=False),
            lax.dynamic_index_in_dim(values, group, 1, keepdims=False),
        ],
        axis=0,
    )
    depth = heads * w_out.shape[1]
    vmem = pl.BlockSpec(memory_space=pltpu.VMEM)
    hbm = pl.BlockSpec(memory_space=pl.ANY)
    dma = pltpu.SemaphoreType.DMA
    context, hidden = pl.pallas_call(
        attend_kernel,
        out_shape=(
            jax.ShapeDtypeStruct((tokens * heads, size), BF16),
            jax.ShapeDtypeStruct((tokens, half), F32),
        ),
        in_specs=[vmem, vmem, hbm, vmem],
        out_specs=(vmem, vmem),
        scratch_shapes=[
            pltpu.VMEM((n, 2 * tokens, size), BF16),
            pltpu.VMEM((n, 2, depth, half), BF16),
            pltpu.VMEM((tokens * heads, size), F32),
            pltpu.VMEM((tokens, heads * size), BF16),
            pltpu.VMEM((2, n // 2, tokens, 2 * depth), BF16),
            pltpu.VMEM((heads * size, 2 * depth), jnp.int32),
            pltpu.VMEM((2, tokens, half), F32),
            dma((15,)), dma((n,)), dma((N_Z, 2)), dma((N_Z, 2)), dma((N_Z, 2)),
            dma((2, N_Z, 2)), dma((n, 2)), dma((1,)), dma((1,)), dma((1,)), dma((1,)),
        ],
        compiler_params=pltpu.CompilerParams(
            collective_id=0, has_side_effects=True, vmem_limit_bytes=50 * 2**20
        ),
        name="attend",
    )(queries.reshape(tokens * heads, size), own_kv, w_out.reshape(depth, 2 * half), resid)

    units = w_down.shape[1]
    rows = n * capacity
    blocks = half // 128
    box = (n, capacity, blocks, 128)
    width = 256
    mixed = pl.pallas_call(
        expert_kernel,
        out_shape=jax.ShapeDtypeStruct((tokens, half), BF16),
        in_specs=[vmem, vmem, vmem, vmem, hbm, hbm],
        out_specs=vmem,
        scratch_shapes=[
            pltpu.VMEM((half, 2 * units), BF16),
            pltpu.VMEM((units, half), BF16),
            pltpu.VMEM((tokens, 128), F32),
            pltpu.VMEM((tokens, 128), F32),
            pltpu.VMEM((rows * blocks, 128), F32),
            pltpu.VMEM((rows, half), BF16),
            pltpu.VMEM(box, BF16), pltpu.VMEM(box, BF16), pltpu.VMEM(box, BF16), pltpu.VMEM(box, BF16),
            pltpu.VMEM((units // width, 2, rows, width), BF16),
            pltpu.VMEM((units // width, 2, rows, width), BF16),
            pltpu.VMEM((rows, units), BF16),
            dma((2,)), dma((units // width,)), dma((units // width,)),
            dma((n,)), dma((n,)), dma((n,)), dma((n,)), dma((2,)),
        ],
        compiler_params=pltpu.CompilerParams(
            collective_id=1, has_side_effects=True, vmem_limit_bytes=50 * 2**20
        ),
        name="experts",
    )(
        hidden, gain.reshape(1, half), pick, mix,
        w_gate_up[0].reshape(half, 2 * units), w_down[0],
    )
    return (context.reshape(tokens, heads, size), mixed)


def solution(mesh):
    in_specs = (
        P("ctx", "exp", None),
        P("ctx", None, None),
        P("ctx", None, None),
        P("ctx", "exp"),
        P("exp"),
        P("ctx", None),
        P("ctx", None),
        P("ctx", "exp", None, None),
        P("ctx", None, "exp"),
        P("exp", "ctx", None),
    )
    out_specs = (P("ctx", "exp", None), P("ctx", "exp"))
    fits = mesh.shape["ctx"] == N_Z * PLANE and mesh.shape["exp"] == 2
    body = fast_body if fits else general_body
    return jax.shard_map(body, mesh=mesh, in_specs=in_specs, out_specs=out_specs, check_vma=False)
```

```python
import functools
import math

import jax
import jax.numpy as jnp
from jax import lax
from jax.experimental import pallas as pl
from jax.experimental.pallas import tpu as pltpu
from jax.sharding import PartitionSpec as P

D = 4096
HQ = 32
KVH = 2
EXPERTS = 128
TOPK = 8


masked_score = -1e30
epsilon = 1e-06


def attend_piece(state_now, pair_piece, offset, query_rows, query_pos, last_pos, scaling):
    key_piece, value_piece = pair_piece
    length = key_piece.shape[0]

    def compute(state_in):
        running, denominator, numerator = state_in
        scores = (
            jnp.einsum("rd,kd->rk", query_rows, key_piece, preferred_element_type=jnp.float32)
            * scaling
        )
        key_pos = jnp.arange(length, dtype=jnp.int32)
        visible = key_pos[None, :] <= query_pos[:, None]
        masked = jnp.where(visible, scores, masked_score)
        highest = jnp.maximum(running, jnp.max(masked, axis=1))
        weights_exp = jnp.where(visible, jnp.exp(masked - highest[:, None]), 0.0)
        rounded = weights_exp.astype(jnp.bfloat16)
        numerator = jnp.dot(rounded, value_piece, preferred_element_type=jnp.float32)
        denominator = jnp.sum(weights_exp, axis=1)
        return (highest, denominator, numerator)

    def untouched(state_in):
        return state_in

    return lax.cond(offset <= last_pos, compute, untouched, state_now)


def general_body(queries, keys, values, resid, gain, expert_ids, gate_scores, w_gate_up, w_down, w_out):
    tokens_here = queries.shape[0]
    heads_here = queries.shape[1]
    head_size = queries.shape[2]
    ctx_count = lax.axis_size("ctx")
    ctx_place = lax.axis_index("ctx")
    exp_place = lax.axis_index("exp")
    own_pos = ctx_place * tokens_here + jnp.arange(tokens_here, dtype=jnp.int32)
    query_sets = (queries, own_pos)
    group_index = exp_place * heads_here // (HQ // KVH)
    key_local = lax.dynamic_index_in_dim(keys, group_index, 1, keepdims=False)
    value_local = lax.dynamic_index_in_dim(values, group_index, 1, keepdims=False)
    scaling = 1.0 / math.sqrt(head_size)
    set_queries, set_pos = query_sets
    set_rows = set_queries.shape[0] * heads_here
    initial = [
        (
            jnp.full((set_rows,), masked_score, jnp.float32),
            jnp.zeros((set_rows,), jnp.float32),
            jnp.zeros((set_rows, head_size), jnp.float32),
        )
    ]
    rows_set = set_queries.reshape(set_rows, head_size)
    pos_set = jnp.repeat(set_pos, heads_here)
    last_set = jnp.max(set_pos)
    updated = [
        attend_piece(
            tuple(initial)[0],
            (
                lax.all_gather(key_local, "ctx", axis=0, tiled=True),
                lax.all_gather(value_local, "ctx", axis=0, tiled=True),
            ),
            jnp.int32(0),
            rows_set,
            pos_set,
            last_set,
            scaling,
        )
    ]
    folded = tuple(updated)
    pieces_out = []
    for state_set in folded:
        normalized = state_set[2] / state_set[1][:, None]
        pieces_out.append(normalized.reshape(-1, heads_here, head_size).astype(jnp.bfloat16))
    context = pieces_out[0]
    whole_out = lax.all_gather(w_out, "ctx", axis=1, tiled=True)
    projected = jnp.einsum("thp,hpd->td", context, whole_out, preferred_element_type=jnp.float32)
    attended = lax.psum_scatter(
        projected.astype(jnp.bfloat16), "exp", scatter_dimension=1, tiled=True
    ).astype(jnp.float32)
    hidden_state = resid.astype(jnp.float32) + attended
    square_sum = lax.psum(jnp.sum(hidden_state * hidden_state, axis=1), "exp")
    inverse = lax.rsqrt(square_sum / D + epsilon)
    normed = (hidden_state * inverse[:, None] * gain[None, :]).astype(jnp.bfloat16)
    capacity = max(2, 5 * tokens_here * TOPK // (4 * EXPERTS))
    flat_ids = expert_ids.reshape(-1)
    onehot = (flat_ids[:, None] == jnp.arange(ctx_count, dtype=jnp.int32)[None, :]).astype(
        jnp.int32
    )
    earlier = jnp.cumsum(onehot, axis=0) - onehot
    rank_of = jnp.sum(earlier * onehot, axis=1)
    active = flat_ids < ctx_count
    slot_of = jnp.where(active, flat_ids * capacity + rank_of, -1).reshape(tokens_here, TOPK)
    slot_range = jnp.arange(ctx_count * capacity, dtype=jnp.int32)
    dispatch_map = jnp.zeros((ctx_count * capacity, tokens_here), jnp.bfloat16)
    for column in range(TOPK):
        dispatch_map = dispatch_map + (slot_range[:, None] == slot_of[None, :, column]).astype(
            jnp.bfloat16
        )
    local_width = normed.shape[1]
    outgoing = jnp.dot(dispatch_map, normed, preferred_element_type=jnp.float32).astype(
        jnp.bfloat16
    )
    outgoing = outgoing.reshape(ctx_count, capacity, local_width)
    arrived = lax.all_to_all(outgoing, "ctx", split_axis=0, concat_axis=0, tiled=True)
    sources = arrived.shape[0]
    width_slots = arrived.shape[1]
    row_block = arrived.reshape(sources * width_slots, local_width)
    partial_sum = jnp.einsum(
        "rd,dgf->rgf", row_block, w_gate_up[0], preferred_element_type=jnp.float32
    )
    summed = lax.psum(partial_sum.astype(jnp.bfloat16), "exp").astype(jnp.float32)
    hidden_units = (jax.nn.silu(summed[:, 0]) * summed[:, 1]).astype(jnp.bfloat16)
    result = jnp.dot(hidden_units, w_down[0], preferred_element_type=jnp.float32).astype(
        jnp.bfloat16
    )
    result = result.reshape(sources, width_slots, local_width)
    returned = lax.all_to_all(result, "ctx", split_axis=0, concat_axis=0, tiled=True)
    back_rows = returned.reshape(ctx_count * capacity, local_width)
    picked = jnp.take(back_rows, jnp.maximum(slot_of, 0).reshape(-1), axis=0).reshape(
        tokens_here, TOPK, local_width
    )
    weight_now = gate_scores / jnp.sum(gate_scores, axis=1, keepdims=True)
    weight_now = jnp.where(active.reshape(tokens_here, TOPK), weight_now, 0.0)
    routed = jnp.zeros((tokens_here, local_width), jnp.float32)
    for column in range(TOPK):
        routed = routed + weight_now[:, column : column + 1] * picked[:, column].astype(jnp.float32)
    mixed = (hidden_state + routed).astype(jnp.bfloat16)
    return (context, mixed)


MESH = pl.DeviceIdType.MESH
F32 = jnp.float32
BF16 = jnp.bfloat16
N_Z = 4
PLANE = 4
HALF_Z = 8


def layer_kernel(
    q_hbm, key_ref, value_ref, w_hbm, resid_hbm, gain_ref, ids_ref, gate_ref, gu_hbm, down_hbm,
    ctx_ref, mixed_ref,
    q_in, resid, kvbuf, wbuf, rows32, ctx2d, ctxbuf, target, acc, part_out, part_in,
    gu_raw, gu, down, squares, peer_squares, hidden_buf, stage, two, outbox, inbox, backbox, endbox,
    parts, peer_parts, act,
    kv_send, kv_recv, own_z, fwd_z, own_y, fwd_y, w_sib, w_recv, x_send, c_send, c_recv, h_send, h_recv,
    sq_sem, p_send, p_recv, a_send, a_recv, b_send, b_recv, local_sem,
):
    c = lax.axis_index("ctx")
    e = lax.axis_index("exp")
    n = inbox.shape[0]
    cap = inbox.shape[1]
    rows = n * cap
    blocks = inbox.shape[2]
    z = c // PLANE
    zh = z // 2
    zl = z % 2
    y = (c // 2) % 2
    k = c % 2
    plane = c % PLANE
    z_peer = c + PLANE * (1 - 2 * zl)
    y_peer = c + 2 * (1 - 2 * y)
    sibling = c + 1 - 2 * k
    partner = c + HALF_Z * (1 - 2 * zh)
    half = resid.shape[1]
    tokens = resid.shape[0]
    heads = q_in.shape[0] // tokens
    wide = wbuf.shape[4]
    depth = wbuf.shape[3]

    def block_of(other_z, other_y, other_k):
        in_z = zl + other_z * (1 - 2 * zl)
        in_y = y + other_y * (1 - 2 * y)
        in_k = k + other_k * (1 - 2 * k)
        return in_z * PLANE + in_y * 2 + in_k

    barrier = pltpu.get_barrier_semaphore()

    @pl.loop(1, n)
    def _(j):
        pl.semaphore_signal(barrier, inc=1, device_id=((c + j) % n, e), device_id_type=MESH)

    pl.semaphore_signal(barrier, inc=1, device_id=(c, 1 - e), device_id_type=MESH)
    mine = block_of(0, 0, 0)

    def own_load(f):
        return pltpu.make_async_copy(
            w_hbm.at[:, pl.ds(pl.multiple_of(e * half + f * wide, wide), wide)],
            wbuf.at[f, mine, e], local_sem.at[f],
        )

    load_q = pltpu.make_async_copy(q_hbm, q_in, local_sem.at[2])
    load_resid = pltpu.make_async_copy(resid_hbm, resid, local_sem.at[3])
    load_gu = pltpu.make_async_copy(gu_hbm, gu_raw, local_sem.at[4])
    load_down = pltpu.make_async_copy(down_hbm, down, local_sem.at[5])
    own_load(0).start()
    own_load(1).start()
    load_q.start()
    load_resid.start()
    load_gu.start()
    load_down.start()
    lane = pl.ds(pl.multiple_of(e * 128, 128), 128)
    kvbuf[c, :tokens, :] = key_ref[:, lane]
    kvbuf[c, tokens:, :] = value_ref[:, lane]
    pl.semaphore_wait(barrier, n)

    def kv_copy(block, slot, to):
        return pltpu.make_async_remote_copy(
            src_ref=kvbuf.at[block], dst_ref=kvbuf.at[block], send_sem=kv_send.at[slot],
            recv_sem=kv_recv.at[block], device_id=(to, e), device_id_type=MESH,
        )

    def w_copy(block, f, g, sem, to):
        return pltpu.make_async_remote_copy(
            src_ref=wbuf.at[f, block, g], dst_ref=wbuf.at[f, block, g], send_sem=sem,
            recv_sem=w_recv.at[block, f, g], device_id=(to, e), device_id_type=MESH,
        )

    def wait_block(block, f, g):
        w_copy(block, f, g, own_z.at[0, 0], sibling).wait_recv()

    def swap(f):
        return pltpu.make_async_remote_copy(
            src_ref=w_hbm.at[:, pl.ds(pl.multiple_of((1 - e) * half + f * wide, wide), wide)],
            dst_ref=wbuf.at[f, mine, e], send_sem=x_send.at[f], recv_sem=w_recv.at[mine, f, e],
            device_id=(c, 1 - e), device_id_type=MESH,
        )

    def group_of(s):
        return (e + s) % 2

    def send_own(f, s):
        g = group_of(s)
        w_copy(mine, f, g, own_z.at[f, g], z_peer).start()
        w_copy(mine, f, g, own_y.at[f, g], y_peer).start()
        w_copy(mine, f, g, w_sib.at[0, f, g], sibling).start()

    for step in range(1, N_Z):
        kv_copy(c, step - 1, ((z + step) % N_Z) * PLANE + plane).start()
    kv_copy(c, 3, y_peer).start()
    kv_copy(c, 7, sibling).start()
    swap(0).start()
    swap(1).start()
    own_load(0).wait()
    send_own(0, 0)
    load_q.wait()
    rows32[...] = q_in[...].astype(F32)
    for step in range(1, N_Z):
        block = ((z + step) % N_Z) * PLANE + plane
        kv_copy(block, 0, sibling).wait_recv()
        kv_copy(block, 3 + step, y_peer).start()
        kv_copy(block, 7 + step, sibling).start()
    wait_block(mine, 0, group_of(1))
    send_own(0, 1)
    own_load(1).wait()
    send_own(1, 0)
    wait_block(mine, 1, group_of(1))
    send_own(1, 1)
    for step in range(N_Z):
        block = ((z + step) % N_Z) * PLANE + (1 - y) * 2 + k
        kv_copy(block, 0, sibling).wait_recv()
        kv_copy(block, 11 + step, sibling).start()
    row = lax.broadcasted_iota(jnp.int32, target.shape, 0)
    col = lax.broadcasted_iota(jnp.int32, target.shape, 1)
    target[...] = row - ((col % 128) // 8) * 128 - (col // 128) * 8 - col % 8
    for block_z in range(N_Z):
        for block_y in range(2):
            kv_copy(block_z * PLANE + block_y * 2 + 1 - k, 0, sibling).wait_recv()

    scale = 1.0 / math.sqrt(q_in.shape[1])
    n_keys = n * tokens

    def attend(pair):
        first = rows32[pl.ds(2 * pair, tokens, stride=heads), :]
        second = rows32[pl.ds(2 * pair + 1, tokens, stride=heads), :]
        both = jnp.concatenate([first, second], axis=0).astype(BF16)
        key_all = kvbuf[:, :tokens, :].reshape(n_keys, 128)
        value_all = kvbuf[:, tokens:, :].reshape(n_keys, 128)
        scores = lax.dot_general(
            both, key_all, (((1,), (1,)), ((), ())), preferred_element_type=F32
        ) * scale
        q_pos = c * tokens + lax.broadcasted_iota(jnp.int32, scores.shape, 0) % tokens
        k_pos = lax.broadcasted_iota(jnp.int32, scores.shape, 1)
        masked = jnp.where(k_pos <= q_pos, scores, masked_score)
        best = jnp.max(masked, axis=1, keepdims=True)
        prob = jnp.exp(masked - best)
        total = jnp.sum(prob, axis=1, keepdims=True)
        part = jnp.dot(prob.astype(BF16), value_all, preferred_element_type=F32)
        done = (part / total).astype(BF16)
        ctx2d[:, pl.ds(pl.multiple_of(pair * 256, 256), 128)] = done[:tokens]
        ctx2d[:, pl.ds(pl.multiple_of(pair * 256 + 128, 128), 128)] = done[tokens:]
        rows32[pl.ds(2 * pair, tokens, stride=heads), :] = done[:tokens].astype(F32)
        rows32[pl.ds(2 * pair + 1, tokens, stride=heads), :] = done[tokens:].astype(F32)

    @pl.loop(0, 2)
    def _(turn):
        @pl.loop(0, heads // 4)
        def _(step):
            attend(turn * (heads // 4) + step)

        @pl.when(turn == 0)
        def _():
            @pl.loop(0, 2)
            def _(s):
                g = group_of(s)
                wait_block(block_of(1, 0, 0), 0, g)
                w_copy(block_of(1, 0, 0), 0, g, fwd_y.at[g], y_peer).start()
                w_copy(block_of(1, 0, 0), 0, g, w_sib.at[1, 0, g], sibling).start()
                wait_block(block_of(0, 1, 0), 0, g)
                w_copy(block_of(0, 1, 0), 0, g, w_sib.at[2, 0, g], sibling).start()

    def pick_pair(pair):
        pick = jnp.where(target[...] == 16 * pair, 1.0, 0.0).astype(BF16)
        return jnp.dot(ctx2d[...], pick, preferred_element_type=F32).astype(BF16)

    n_pairs = ctxbuf.shape[2]

    @pl.loop(0, n_pairs)
    def _(pair):
        ctxbuf[2, 0, pair] = pick_pair((1 - zh) * n_pairs + pair)

    def ctx_copy(slot, src, dst, to):
        return pltpu.make_async_remote_copy(
            src_ref=src, dst_ref=dst, send_sem=c_send.at[slot], recv_sem=c_recv.at[slot],
            device_id=to, device_id_type=MESH,
        )

    to_partner = ctx_copy(0, ctxbuf.at[2, 0], ctxbuf.at[1, e], (partner, e))
    to_partner.start()

    @pl.loop(0, n_pairs)
    def _(pair):
        ctxbuf[0, e, pair] = pick_pair(zh * n_pairs + pair)

    own_over = ctx_copy(1, ctxbuf.at[0, e], ctxbuf.at[0, e], (c, 1 - e))
    own_over.start()

    @pl.loop(0, 2)
    def _(s):
        g = group_of(s)
        wait_block(block_of(0, 1, 0), 1, g)
        w_copy(block_of(0, 1, 0), 1, g, fwd_z.at[g], z_peer).start()
        w_copy(block_of(0, 1, 0), 1, g, w_sib.at[2, 1, g], sibling).start()
        wait_block(block_of(1, 0, 0), 1, g)
        w_copy(block_of(1, 0, 0), 1, g, w_sib.at[1, 1, g], sibling).start()

    units = down.shape[0]
    unpack_rows = 128

    def unpack(first, count):
        @pl.loop(first, first + count)
        def _(i):
            at = pl.ds(pl.multiple_of(i * unpack_rows, unpack_rows), unpack_rows)
            gu[at, :units] = gu_raw[at, 0, :]
            gu[at, units:] = gu_raw[at, 1, :]

    n_unpack = half // unpack_rows
    load_gu.wait()
    unpack(0, n_unpack // 4)
    pltpu.make_async_remote_copy(
        src_ref=ctxbuf.at[1, e], dst_ref=ctxbuf.at[1, e], send_sem=c_send.at[0],
        recv_sem=c_recv.at[0], device_id=(partner, e), device_id_type=MESH,
    ).wait_recv()
    partner_over = ctx_copy(2, ctxbuf.at[1, e], ctxbuf.at[1, e], (c, 1 - e))
    partner_over.start()

    def relay_far(f):
        @pl.loop(0, 2)
        def _(s):
            g = group_of(s)
            wait_block(block_of(1, 1, 0), f, g)
            w_copy(block_of(1, 1, 0), f, g, w_sib.at[3, f, g], sibling).start()

    relay_far(0)
    unpack(n_unpack // 4, n_unpack // 4)
    ctx_ref[...] = rows32[...].astype(BF16)
    acc[...] = jnp.zeros_like(acc)
    for slot in range(2):
        pltpu.make_async_remote_copy(
            src_ref=ctxbuf.at[slot, 1 - e], dst_ref=ctxbuf.at[slot, 1 - e], send_sem=c_send.at[0],
            recv_sem=c_recv.at[1 + slot], device_id=(c, 1 - e), device_id_type=MESH,
        ).wait_recv()

    def project(f):
        @pl.loop(0, 8)
        def _(i):
            other_z = i // 4
            other_y = (i // 2) % 2
            g = group_of(i % 2)
            wait_block(block_of(other_z, other_y, 1), f, g)
            first = block_of(other_z, other_y, 0)
            pair = first // 2
            weights = wbuf[f, pl.ds(2 * pair, 2), pl.ds(g, 1)].reshape(2 * depth, wide)
            lhs = jnp.concatenate([ctxbuf[0, g, pair], ctxbuf[1, g, pair]], axis=0)
            acc[f] += jnp.dot(lhs, weights, preferred_element_type=F32)

        part_out[f] = acc[f, tokens:, :].astype(BF16)
        pltpu.make_async_remote_copy(
            src_ref=part_out.at[f], dst_ref=part_in.at[f], send_sem=h_send.at[f],
            recv_sem=h_recv.at[f], device_id=(partner, e), device_id_type=MESH,
        ).start()

    def part_copy(f):
        return pltpu.make_async_remote_copy(
            src_ref=part_out.at[f], dst_ref=part_in.at[f], send_sem=h_send.at[f],
            recv_sem=h_recv.at[f], device_id=(partner, e), device_id_type=MESH,
        )

    project(0)
    relay_far(1)
    project(1)
    load_resid.wait()
    unpack(n_unpack // 2, n_unpack // 4)

    slot = lax.broadcasted_iota(jnp.int32, (tokens, rows), 1)
    named = jnp.zeros((tokens, rows), F32)
    share = jnp.zeros((tokens, rows), F32)
    gates = gate_ref[...]
    gates = gates / jnp.sum(gates, axis=1, keepdims=True)
    for column in range(TOPK):
        hit = ids_ref[:, column : column + 1] == slot // cap
        named = jnp.where(hit, 1.0, named)
        share = jnp.where(hit, gates[:, column : column + 1], share)
    before = jnp.where(
        lax.broadcasted_iota(jnp.int32, (tokens, tokens), 1)
        < lax.broadcasted_iota(jnp.int32, (tokens, tokens), 0),
        1.0,
        0.0,
    ).astype(BF16)
    rank = jnp.dot(before, named.astype(BF16), preferred_element_type=F32)
    chosen = jnp.logical_and(named > 0.5, rank == (slot % cap).astype(F32))
    pick = jnp.where(chosen, 1.0, 0.0).astype(BF16)
    mix = jnp.where(chosen, share, 0.0)
    mix_high = mix.astype(BF16)
    mix_low = (mix - mix_high.astype(F32)).astype(BF16)

    own = jnp.zeros((tokens, 1), F32)
    for f in range(2):
        part_copy(f).wait_recv()
        at = pl.ds(f * wide, wide)
        state = resid[:, at].astype(F32) + (acc[f, :tokens, :] + part_in[f].astype(F32))
        hidden_buf[:, at] = state
        own += jnp.sum(state * state, axis=1, keepdims=True)
    squares[...] = jnp.broadcast_to(own, squares.shape)
    sq = pltpu.make_async_remote_copy(
        src_ref=squares, dst_ref=peer_squares, send_sem=sq_sem.at[0], recv_sem=sq_sem.at[1],
        device_id=(c, 1 - e), device_id_type=MESH,
    )
    sq.start()
    sq.wait()
    mean = (squares[:, :1] + peer_squares[:, :1]) / D
    normed = (hidden_buf[...] * lax.rsqrt(mean + epsilon) * gain_ref[...]).astype(BF16)
    two[:tokens, :] = normed
    for j in range(blocks // 2):
        sent = lax.dot_general(
            pick, two[:tokens, j * 256 : (j + 1) * 256], (((0,), (0,)), ((), ())),
            preferred_element_type=F32,
        )
        stage[pl.ds(2 * j, rows, stride=blocks), :] = sent[:, :128]
        stage[pl.ds(2 * j + 1, rows, stride=blocks), :] = sent[:, 128:]
    outbox[...] = stage[...].reshape(outbox.shape).astype(BF16)

    def a_copy(j):
        to = (c + j) % n
        return pltpu.make_async_remote_copy(
            src_ref=outbox.at[to], dst_ref=inbox.at[c], send_sem=a_send.at[j],
            recv_sem=a_recv.at[c], device_id=(to, e), device_id_type=MESH,
        )

    def b_copy(j):
        to = (c + j) % n
        return pltpu.make_async_remote_copy(
            src_ref=backbox.at[to], dst_ref=endbox.at[c], send_sem=b_send.at[j],
            recv_sem=b_recv.at[c], device_id=(to, e), device_id_type=MESH,
        )

    def arrived(box, sems):
        @pl.loop(1, n)
        def _(j):
            source = (c + j) % n
            pltpu.make_async_remote_copy(
                src_ref=box.at[source], dst_ref=box.at[source], send_sem=a_send.at[0],
                recv_sem=sems.at[source], device_id=(source, e), device_id_type=MESH,
            ).wait_recv()

        stage[...] = box[...].reshape(stage.shape).astype(F32)
        for j in range(blocks):
            two[:, j * 128 : (j + 1) * 128] = stage[pl.ds(j, rows, stride=blocks), :].astype(BF16)

    @pl.loop(1, n)
    def _(j):
        a_copy(j).start()

    inbox[c] = outbox[c]
    unpack(3 * (n_unpack // 4), n_unpack // 4)
    arrived(inbox, a_recv)
    width = parts.shape[3]

    def p_copy(m):
        return pltpu.make_async_remote_copy(
            src_ref=parts.at[m], dst_ref=peer_parts.at[m], send_sem=p_send.at[m],
            recv_sem=p_recv.at[m], device_id=(c, 1 - e), device_id_type=MESH,
        )

    n_parts = units // width
    for m in range(n_parts):
        for side in range(2):
            start = side * units + m * width
            parts[m, side] = jnp.dot(
                two[...], gu[:, start : start + width], preferred_element_type=F32
            ).astype(BF16)
        p_copy(m).start()
    for m in range(n_parts):
        p_copy(m).wait_recv()
        gate = parts[m, 0].astype(F32) + peer_parts[m, 0].astype(F32)
        up = parts[m, 1].astype(F32) + peer_parts[m, 1].astype(F32)
        act[:, m * width : (m + 1) * width] = (gate / (1.0 + jnp.exp(-gate)) * up).astype(BF16)
    load_down.wait()
    for j in range(blocks // 2):
        result = jnp.dot(
            act[...], down[:, j * 256 : (j + 1) * 256], preferred_element_type=F32
        )
        stage[pl.ds(2 * j, rows, stride=blocks), :] = result[:, :128]
        stage[pl.ds(2 * j + 1, rows, stride=blocks), :] = result[:, 128:]
    backbox[...] = stage[...].reshape(backbox.shape).astype(BF16)

    @pl.loop(1, n)
    def _(j):
        b_copy(j).start()

    endbox[c] = backbox[c]
    arrived(endbox, b_recv)
    routed = jnp.dot(mix_high, two[...], preferred_element_type=F32)
    routed += jnp.dot(mix_low, two[...], preferred_element_type=F32)
    mixed_ref[...] = (hidden_buf[...] + routed).astype(BF16)

    for slot_index in range(15):
        kv_copy(c, slot_index, sibling).wait_send()
    for f in range(2):
        swap(f).wait_send()
        part_copy(f).wait_send()
    to_partner.wait_send()
    own_over.wait_send()
    partner_over.wait_send()

    @pl.loop(0, 2)
    def _(g):
        w_copy(mine, 0, g, fwd_y.at[g], sibling).wait_send()
        w_copy(mine, 0, g, fwd_z.at[g], sibling).wait_send()
        for f in range(2):
            w_copy(mine, f, g, own_z.at[f, g], sibling).wait_send()
            w_copy(mine, f, g, own_y.at[f, g], sibling).wait_send()
            for source in range(4):
                w_copy(mine, f, g, w_sib.at[source, f, g], sibling).wait_send()

    @pl.loop(1, n)
    def _(j):
        a_copy(j).wait_send()
        b_copy(j).wait_send()

    for m in range(n_parts):
        p_copy(m).wait_send()


def fast_body(queries, keys, values, resid, gain, expert_ids, gate_scores, w_gate_up, w_down, w_out):
    tokens, heads, size = queries.shape
    n = lax.axis_size("ctx")
    half = resid.shape[1]
    wide = half // 2
    capacity = max(2, 5 * tokens * TOPK // (4 * EXPERTS))
    depth = heads * w_out.shape[1]
    units = w_down.shape[1]
    rows = n * capacity
    blocks = half // 128
    box = (n, capacity, blocks, 128)
    width = 256
    vmem = pl.BlockSpec(memory_space=pltpu.VMEM)
    hbm = pl.BlockSpec(memory_space=pl.ANY)
    dma = pltpu.SemaphoreType.DMA
    context, mixed = pl.pallas_call(
        layer_kernel,
        out_shape=(
            jax.ShapeDtypeStruct((tokens * heads, size), BF16),
            jax.ShapeDtypeStruct((tokens, half), BF16),
        ),
        in_specs=[hbm, vmem, vmem, hbm, hbm, vmem, vmem, vmem, hbm, hbm],
        out_specs=(vmem, vmem),
        scratch_shapes=[
            pltpu.VMEM((tokens * heads, size), BF16),
            pltpu.VMEM((tokens, half), BF16),
            pltpu.VMEM((n, 2 * tokens, size), BF16),
            pltpu.VMEM((2, HALF_Z, 2, depth, wide), BF16),
            pltpu.VMEM((tokens * heads, size), F32),
            pltpu.VMEM((tokens, heads * size), BF16),
            pltpu.VMEM((3, 2, HALF_Z // 2, tokens, 2 * depth), BF16),
            pltpu.VMEM((heads * size, 2 * depth), jnp.int32),
            pltpu.VMEM((2, 2 * tokens, wide), F32),
            pltpu.VMEM((2, tokens, wide), BF16),
            pltpu.VMEM((2, tokens, wide), BF16),
            pltpu.VMEM((half, 2, units), BF16),
            pltpu.VMEM((half, 2 * units), BF16),
            pltpu.VMEM((units, half), BF16),
            pltpu.VMEM((tokens, 128), F32),
            pltpu.VMEM((tokens, 128), F32),
            pltpu.VMEM((tokens, half), F32),
            pltpu.VMEM((rows * blocks, 128), F32),
            pltpu.VMEM((rows, half), BF16),
            pltpu.VMEM(box, BF16), pltpu.VMEM(box, BF16), pltpu.VMEM(box, BF16), pltpu.VMEM(box, BF16),
            pltpu.VMEM((units // width, 2, rows, width), BF16),
            pltpu.VMEM((units // width, 2, rows, width), BF16),
            pltpu.VMEM((rows, units), BF16),
            dma((15,)), dma((n,)), dma((2, 2)), dma((2,)), dma((2, 2)), dma((2,)),
            dma((4, 2, 2)), dma((HALF_Z, 2, 2)), dma((2,)), dma((3,)), dma((3,)), dma((2,)), dma((2,)),
            dma((2,)), dma((units // width,)), dma((units // width,)),
            dma((n,)), dma((n,)), dma((n,)), dma((n,)), dma((6,)),
        ],
        compiler_params=pltpu.CompilerParams(
            collective_id=0, has_side_effects=True, vmem_limit_bytes=56 * 2**20
        ),
        name="layer",
    )(
        queries.reshape(tokens * heads, size), keys.reshape(tokens, -1), values.reshape(tokens, -1),
        w_out.reshape(depth, 2 * half), resid, gain.reshape(1, half), expert_ids, gate_scores,
        w_gate_up[0], w_down[0],
    )
    return (context.reshape(tokens, heads, size), mixed)


def solution(mesh):
    in_specs = (
        P("ctx", "exp", None),
        P("ctx", None, None),
        P("ctx", None, None),
        P("ctx", "exp"),
        P("exp"),
        P("ctx", None),
        P("ctx", None),
        P("ctx", "exp", None, None),
        P("ctx", None, "exp"),
        P("exp", "ctx", None),
    )
    out_specs = (P("ctx", "exp", None), P("ctx", "exp"))
    fits = mesh.shape["ctx"] == N_Z * PLANE and mesh.shape["exp"] == 2
    body = fast_body if fits else general_body
    return jax.shard_map(body, mesh=mesh, in_specs=in_specs, out_specs=out_specs, check_vma=False)
```

```python
import functools
import math

import jax
import jax.numpy as jnp
from jax import lax
from jax.experimental import pallas as pl
from jax.experimental.pallas import tpu as pltpu
from jax.sharding import PartitionSpec as P

D = 4096
HQ = 32
KVH = 2
EXPERTS = 128
TOPK = 8


masked_score = -1e30
epsilon = 1e-06


def attend_piece(state_now, pair_piece, offset, query_rows, query_pos, last_pos, scaling):
    key_piece, value_piece = pair_piece
    length = key_piece.shape[0]

    def compute(state_in):
        running, denominator, numerator = state_in
        scores = (
            jnp.einsum("rd,kd->rk", query_rows, key_piece, preferred_element_type=jnp.float32)
            * scaling
        )
        key_pos = jnp.arange(length, dtype=jnp.int32)
        visible = key_pos[None, :] <= query_pos[:, None]
        masked = jnp.where(visible, scores, masked_score)
        highest = jnp.maximum(running, jnp.max(masked, axis=1))
        weights_exp = jnp.where(visible, jnp.exp(masked - highest[:, None]), 0.0)
        rounded = weights_exp.astype(jnp.bfloat16)
        numerator = jnp.dot(rounded, value_piece, preferred_element_type=jnp.float32)
        denominator = jnp.sum(weights_exp, axis=1)
        return (highest, denominator, numerator)

    def untouched(state_in):
        return state_in

    return lax.cond(offset <= last_pos, compute, untouched, state_now)


def general_body(queries, keys, values, resid, gain, expert_ids, gate_scores, w_gate_up, w_down, w_out):
    tokens_here = queries.shape[0]
    heads_here = queries.shape[1]
    head_size = queries.shape[2]
    ctx_count = lax.axis_size("ctx")
    ctx_place = lax.axis_index("ctx")
    exp_place = lax.axis_index("exp")
    own_pos = ctx_place * tokens_here + jnp.arange(tokens_here, dtype=jnp.int32)
    query_sets = (queries, own_pos)
    group_index = exp_place * heads_here // (HQ // KVH)
    key_local = lax.dynamic_index_in_dim(keys, group_index, 1, keepdims=False)
    value_local = lax.dynamic_index_in_dim(values, group_index, 1, keepdims=False)
    scaling = 1.0 / math.sqrt(head_size)
    set_queries, set_pos = query_sets
    set_rows = set_queries.shape[0] * heads_here
    initial = [
        (
            jnp.full((set_rows,), masked_score, jnp.float32),
            jnp.zeros((set_rows,), jnp.float32),
            jnp.zeros((set_rows, head_size), jnp.float32),
        )
    ]
    rows_set = set_queries.reshape(set_rows, head_size)
    pos_set = jnp.repeat(set_pos, heads_here)
    last_set = jnp.max(set_pos)
    updated = [
        attend_piece(
            tuple(initial)[0],
            (
                lax.all_gather(key_local, "ctx", axis=0, tiled=True),
                lax.all_gather(value_local, "ctx", axis=0, tiled=True),
            ),
            jnp.int32(0),
            rows_set,
            pos_set,
            last_set,
            scaling,
        )
    ]
    folded = tuple(updated)
    pieces_out = []
    for state_set in folded:
        normalized = state_set[2] / state_set[1][:, None]
        pieces_out.append(normalized.reshape(-1, heads_here, head_size).astype(jnp.bfloat16))
    context = pieces_out[0]
    whole_out = lax.all_gather(w_out, "ctx", axis=1, tiled=True)
    projected = jnp.einsum("thp,hpd->td", context, whole_out, preferred_element_type=jnp.float32)
    attended = lax.psum_scatter(
        projected.astype(jnp.bfloat16), "exp", scatter_dimension=1, tiled=True
    ).astype(jnp.float32)
    hidden_state = resid.astype(jnp.float32) + attended
    square_sum = lax.psum(jnp.sum(hidden_state * hidden_state, axis=1), "exp")
    inverse = lax.rsqrt(square_sum / D + epsilon)
    normed = (hidden_state * inverse[:, None] * gain[None, :]).astype(jnp.bfloat16)
    capacity = max(2, 5 * tokens_here * TOPK // (4 * EXPERTS))
    flat_ids = expert_ids.reshape(-1)
    onehot = (flat_ids[:, None] == jnp.arange(ctx_count, dtype=jnp.int32)[None, :]).astype(
        jnp.int32
    )
    earlier = jnp.cumsum(onehot, axis=0) - onehot
    rank_of = jnp.sum(earlier * onehot, axis=1)
    active = flat_ids < ctx_count
    slot_of = jnp.where(active, flat_ids * capacity + rank_of, -1).reshape(tokens_here, TOPK)
    slot_range = jnp.arange(ctx_count * capacity, dtype=jnp.int32)
    dispatch_map = jnp.zeros((ctx_count * capacity, tokens_here), jnp.bfloat16)
    for column in range(TOPK):
        dispatch_map = dispatch_map + (slot_range[:, None] == slot_of[None, :, column]).astype(
            jnp.bfloat16
        )
    local_width = normed.shape[1]
    outgoing = jnp.dot(dispatch_map, normed, preferred_element_type=jnp.float32).astype(
        jnp.bfloat16
    )
    outgoing = outgoing.reshape(ctx_count, capacity, local_width)
    arrived = lax.all_to_all(outgoing, "ctx", split_axis=0, concat_axis=0, tiled=True)
    sources = arrived.shape[0]
    width_slots = arrived.shape[1]
    row_block = arrived.reshape(sources * width_slots, local_width)
    partial_sum = jnp.einsum(
        "rd,dgf->rgf", row_block, w_gate_up[0], preferred_element_type=jnp.float32
    )
    summed = lax.psum(partial_sum.astype(jnp.bfloat16), "exp").astype(jnp.float32)
    hidden_units = (jax.nn.silu(summed[:, 0]) * summed[:, 1]).astype(jnp.bfloat16)
    result = jnp.dot(hidden_units, w_down[0], preferred_element_type=jnp.float32).astype(
        jnp.bfloat16
    )
    result = result.reshape(sources, width_slots, local_width)
    returned = lax.all_to_all(result, "ctx", split_axis=0, concat_axis=0, tiled=True)
    back_rows = returned.reshape(ctx_count * capacity, local_width)
    picked = jnp.take(back_rows, jnp.maximum(slot_of, 0).reshape(-1), axis=0).reshape(
        tokens_here, TOPK, local_width
    )
    weight_now = gate_scores / jnp.sum(gate_scores, axis=1, keepdims=True)
    weight_now = jnp.where(active.reshape(tokens_here, TOPK), weight_now, 0.0)
    routed = jnp.zeros((tokens_here, local_width), jnp.float32)
    for column in range(TOPK):
        routed = routed + weight_now[:, column : column + 1] * picked[:, column].astype(jnp.float32)
    mixed = (hidden_state + routed).astype(jnp.bfloat16)
    return (context, mixed)


MESH = pl.DeviceIdType.MESH
F32 = jnp.float32
BF16 = jnp.bfloat16
N_Z = 4
PLANE = 4
HALF_Z = 8


def layer_kernel(
    q_hbm, key_hbm, value_hbm, w_hbm, resid_hbm, gain_hbm, ids_hbm, gate_hbm, gu_hbm, down_hbm,
    ctx_ref, mixed_ref,
    key_ref, value_ref, gain_ref, ids_ref, gate_ref, q_in, resid, kvbuf, wbuf, rows32, ctx2d, ctxbuf, target, acc, part_out, part_in,
    gu_raw, gu, down, squares, peer_squares, hidden_buf, stage, two, outbox, inbox, backbox, endbox,
    parts, peer_parts, act, mixes, normed_buf,
    kv_send, kv_recv, own_z, fwd_z, own_y, fwd_y, w_sib, w_recv, x_send, c_send, c_recv, h_send, h_recv,
    sq_sem, p_send, p_recv, a_send, a_recv, b_send, b_recv, local_sem,
):
    c = lax.axis_index("ctx")
    e = lax.axis_index("exp")
    n = inbox.shape[0]
    cap = inbox.shape[1]
    rows = n * cap
    blocks = inbox.shape[2]
    z = c // PLANE
    zh = z // 2
    zl = z % 2
    y = (c // 2) % 2
    k = c % 2
    plane = c % PLANE
    z_peer = c + PLANE * (1 - 2 * zl)
    y_peer = c + 2 * (1 - 2 * y)
    sibling = c + 1 - 2 * k
    partner = c + HALF_Z * (1 - 2 * zh)
    half = resid.shape[1]
    tokens = resid.shape[0]
    heads = q_in.shape[0] // tokens
    wide = wbuf.shape[4]
    depth = wbuf.shape[3]

    def block_of(other_z, other_y, other_k):
        in_z = zl + other_z * (1 - 2 * zl)
        in_y = y + other_y * (1 - 2 * y)
        in_k = k + other_k * (1 - 2 * k)
        return in_z * PLANE + in_y * 2 + in_k

    barrier = pltpu.get_barrier_semaphore()

    @pl.loop(1, n)
    def _(j):
        pl.semaphore_signal(barrier, inc=1, device_id=((c + j) % n, e), device_id_type=MESH)

    pl.semaphore_signal(barrier, inc=1, device_id=(c, 1 - e), device_id_type=MESH)
    mine = block_of(0, 0, 0)

    def own_load(f):
        return pltpu.make_async_copy(
            w_hbm.at[:, pl.ds(pl.multiple_of(e * half + f * wide, wide), wide)],
            wbuf.at[f, mine, e], local_sem.at[f],
        )

    load_q = pltpu.make_async_copy(q_hbm, q_in, local_sem.at[2])
    load_resid = pltpu.make_async_copy(resid_hbm, resid, local_sem.at[3])
    load_gu = pltpu.make_async_copy(gu_hbm, gu_raw, local_sem.at[4])
    load_down = pltpu.make_async_copy(down_hbm, down, local_sem.at[5])
    small = [
        pltpu.make_async_copy(source, held, local_sem.at[6 + i])
        for i, (source, held) in enumerate(
            (
                (key_hbm, key_ref), (value_hbm, value_ref), (gain_hbm, gain_ref),
                (ids_hbm, ids_ref), (gate_hbm, gate_ref),
            )
        )
    ]
    for copy in small:
        copy.start()
    own_load(0).start()
    own_load(1).start()
    load_q.start()
    load_resid.start()
    load_gu.start()
    load_down.start()
    small[0].wait()
    small[1].wait()
    group = e * heads // (HQ // KVH)
    for part, source in enumerate((key_ref, value_ref)):
        picked = jnp.where(group == 0, source[:, 0, :].astype(F32), source[:, 1, :].astype(F32))
        kvbuf[c, part * tokens : (part + 1) * tokens, :] = picked.astype(BF16)
    pl.semaphore_wait(barrier, n)

    def kv_copy(block, slot, to):
        return pltpu.make_async_remote_copy(
            src_ref=kvbuf.at[block], dst_ref=kvbuf.at[block], send_sem=kv_send.at[slot],
            recv_sem=kv_recv.at[block], device_id=(to, e), device_id_type=MESH,
        )

    def w_copy(block, f, g, sem, to):
        return pltpu.make_async_remote_copy(
            src_ref=wbuf.at[f, block, g], dst_ref=wbuf.at[f, block, g], send_sem=sem,
            recv_sem=w_recv.at[block, f, g], device_id=(to, e), device_id_type=MESH,
        )

    def wait_block(block, f, g):
        w_copy(block, f, g, own_z.at[0, 0], sibling).wait_recv()

    def swap(f):
        return pltpu.make_async_remote_copy(
            src_ref=w_hbm.at[:, pl.ds(pl.multiple_of((1 - e) * half + f * wide, wide), wide)],
            dst_ref=wbuf.at[f, mine, e], send_sem=x_send.at[f], recv_sem=w_recv.at[mine, f, e],
            device_id=(c, 1 - e), device_id_type=MESH,
        )

    def group_of(s):
        return (e + s) % 2

    def send_own(f, s):
        g = group_of(s)
        w_copy(mine, f, g, own_z.at[f, g], z_peer).start()
        w_copy(mine, f, g, own_y.at[f, g], y_peer).start()
        w_copy(mine, f, g, w_sib.at[0, f, g], sibling).start()

    for step in range(1, N_Z):
        kv_copy(c, step - 1, ((z + step) % N_Z) * PLANE + plane).start()
    kv_copy(c, 3, y_peer).start()
    kv_copy(c, 7, sibling).start()
    swap(0).start()
    swap(1).start()
    load_q.wait()
    rows32[...] = q_in[...].astype(F32)
    for step in range(1, N_Z):
        block = ((z + step) % N_Z) * PLANE + plane
        kv_copy(block, 0, sibling).wait_recv()
        kv_copy(block, 3 + step, y_peer).start()
        kv_copy(block, 7 + step, sibling).start()
    own_load(0).wait()
    send_own(0, 0)
    wait_block(mine, 0, group_of(1))
    send_own(0, 1)
    own_load(1).wait()
    send_own(1, 0)
    wait_block(mine, 1, group_of(1))
    send_own(1, 1)
    for step in range(N_Z):
        block = ((z + step) % N_Z) * PLANE + (1 - y) * 2 + k
        kv_copy(block, 0, sibling).wait_recv()
        kv_copy(block, 11 + step, sibling).start()
    depth_part = depth // 2
    row = lax.broadcasted_iota(jnp.int32, target.shape, 0)
    col = lax.broadcasted_iota(jnp.int32, target.shape, 1)
    target[...] = row - ((col % depth_part) // 8) * 128 - (col // depth_part) * 8 - col % 8
    for block_z in range(N_Z):
        for block_y in range(2):
            kv_copy(block_z * PLANE + block_y * 2 + 1 - k, 0, sibling).wait_recv()

    scale = math.log2(math.e) / math.sqrt(q_in.shape[1])
    n_keys = n * tokens

    def attend(pair):
        first = rows32[pl.ds(2 * pair, tokens, stride=heads), :]
        second = rows32[pl.ds(2 * pair + 1, tokens, stride=heads), :]
        both = jnp.concatenate([first, second], axis=0).astype(BF16)
        key_all = kvbuf[:, :tokens, :].reshape(n_keys, 128)
        value_all = kvbuf[:, tokens:, :].reshape(n_keys, 128)
        scores = lax.dot_general(
            both, key_all, (((1,), (1,)), ((), ())), preferred_element_type=F32
        )
        q_pos = c * tokens + lax.broadcasted_iota(jnp.int32, scores.shape, 0) % tokens
        k_pos = lax.broadcasted_iota(jnp.int32, scores.shape, 1)
        masked = jnp.where(k_pos <= q_pos, scores, masked_score)
        best = jnp.max(masked, axis=1, keepdims=True)
        prob = jnp.exp2((masked - best) * scale)
        total = jnp.sum(prob, axis=1, keepdims=True)
        part = jnp.dot(prob.astype(BF16), value_all, preferred_element_type=F32)
        done = (part / total).astype(BF16)
        turn = pair // (heads // 4)
        at = pair % (heads // 4) * 256
        ctx2d[turn, :, pl.ds(pl.multiple_of(at, 256), 128)] = done[:tokens]
        ctx2d[turn, :, pl.ds(pl.multiple_of(at + 128, 128), 128)] = done[tokens:]
        rows32[pl.ds(2 * pair, tokens, stride=heads), :] = done[:tokens].astype(F32)
        rows32[pl.ds(2 * pair + 1, tokens, stride=heads), :] = done[tokens:].astype(F32)

    def ctx_copy(slot, hh, src, dst, to):
        return pltpu.make_async_remote_copy(
            src_ref=src, dst_ref=dst, send_sem=c_send.at[slot, hh], recv_sem=c_recv.at[slot, hh],
            device_id=to, device_id_type=MESH,
        )

    def to_partner(hh):
        return ctx_copy(0, hh, ctxbuf.at[2, 0, hh], ctxbuf.at[1, e, hh], (partner, e))

    def over(slot, hh):
        return ctx_copy(1 + slot, hh, ctxbuf.at[slot, e, hh], ctxbuf.at[slot, e, hh], (c, 1 - e))

    def pass_on(hh):
        ctx_copy(0, hh, ctxbuf.at[1, e, hh], ctxbuf.at[1, e, hh], (partner, e)).wait_recv()
        over(1, hh).start()

    def pick_quad(hh, quad):
        pick = jnp.where(target[...] == 32 * quad, 1.0, 0.0).astype(BF16)
        return jnp.dot(ctx2d[hh], pick, preferred_element_type=F32).astype(BF16)

    @pl.loop(0, 2)
    def _(turn):
        @pl.loop(0, heads // 4)
        def _(step):
            attend(turn * (heads // 4) + step)

        @pl.loop(0, 2)
        def _(quad):
            ctxbuf[2, 0, turn, quad] = pick_quad(turn, (1 - zh) * 2 + quad)

        to_partner(turn).start()

        @pl.loop(0, 2)
        def _(quad):
            ctxbuf[0, e, turn, quad] = pick_quad(turn, zh * 2 + quad)

        over(0, turn).start()

        @pl.when(turn == 0)
        def _():
            @pl.loop(0, 2)
            def _(s):
                g = group_of(s)
                wait_block(block_of(1, 0, 0), 0, g)
                w_copy(block_of(1, 0, 0), 0, g, fwd_y.at[g], y_peer).start()
                w_copy(block_of(1, 0, 0), 0, g, w_sib.at[1, 0, g], sibling).start()
                wait_block(block_of(0, 1, 0), 0, g)
                w_copy(block_of(0, 1, 0), 0, g, w_sib.at[2, 0, g], sibling).start()

    pass_on(0)

    @pl.loop(0, 2)
    def _(s):
        g = group_of(s)
        wait_block(block_of(0, 1, 0), 1, g)
        w_copy(block_of(0, 1, 0), 1, g, fwd_z.at[g], z_peer).start()
        w_copy(block_of(0, 1, 0), 1, g, w_sib.at[2, 1, g], sibling).start()
        wait_block(block_of(1, 0, 0), 1, g)
        w_copy(block_of(1, 0, 0), 1, g, w_sib.at[1, 1, g], sibling).start()

    units = down.shape[0]
    unpack_rows = 128

    def unpack(first, count):
        @pl.loop(first, first + count)
        def _(i):
            at = pl.ds(pl.multiple_of(i * unpack_rows, unpack_rows), unpack_rows)
            gu[at, :units] = gu_raw[at, 0, :]
            gu[at, units:] = gu_raw[at, 1, :]

    n_unpack = half // unpack_rows
    load_gu.wait()
    unpack(0, n_unpack // 4)
    pass_on(1)

    def relay_far(f):
        @pl.loop(0, 2)
        def _(s):
            g = group_of(s)
            wait_block(block_of(1, 1, 0), f, g)
            w_copy(block_of(1, 1, 0), f, g, w_sib.at[3, f, g], sibling).start()

    relay_far(0)
    unpack(n_unpack // 4, n_unpack // 4)
    ctx_ref[...] = rows32[...].astype(BF16)
    acc[...] = jnp.zeros_like(acc)
    for hh in range(2):
        for slot in range(2):
            ctx_copy(
                1 + slot, hh, ctxbuf.at[slot, 1 - e, hh], ctxbuf.at[slot, 1 - e, hh], (c, 1 - e)
            ).wait_recv()

    def project(f):
        @pl.loop(0, 4)
        def _(i):
            other_z = i // 2
            g = group_of(i % 2)
            wait_block(block_of(other_z, 0, 1), f, g)
            wait_block(block_of(other_z, 1, 1), f, g)
            quad = zl + other_z * (1 - 2 * zl)
            for hh in range(2):
                weights = wbuf[
                    f, pl.ds(quad * PLANE, PLANE), pl.ds(g, 1), hh * depth_part : (hh + 1) * depth_part
                ].reshape(PLANE * depth_part, wide)
                lhs = jnp.concatenate([ctxbuf[0, g, hh, quad], ctxbuf[1, g, hh, quad]], axis=0)
                acc[f] += jnp.dot(lhs, weights, preferred_element_type=F32)

        part_out[f] = acc[f, tokens:, :].astype(BF16)
        pltpu.make_async_remote_copy(
            src_ref=part_out.at[f], dst_ref=part_in.at[f], send_sem=h_send.at[f],
            recv_sem=h_recv.at[f], device_id=(partner, e), device_id_type=MESH,
        ).start()

    def part_copy(f):
        return pltpu.make_async_remote_copy(
            src_ref=part_out.at[f], dst_ref=part_in.at[f], send_sem=h_send.at[f],
            recv_sem=h_recv.at[f], device_id=(partner, e), device_id_type=MESH,
        )

    project(0)
    relay_far(1)
    project(1)
    load_resid.wait()
    unpack(n_unpack // 2, n_unpack // 4)

    for copy in small[2:]:
        copy.wait()
    slot = lax.broadcasted_iota(jnp.int32, (rows, tokens), 0)
    named = jnp.zeros((rows, tokens), F32)
    share = jnp.zeros((rows, tokens), F32)
    gates = gate_ref[...]
    gates = gates / jnp.sum(gates, axis=0, keepdims=True)
    for column in range(TOPK):
        hit = ids_ref[column : column + 1, :] == slot // cap
        named = jnp.where(hit, 1.0, named)
        share = jnp.where(hit, gates[column : column + 1, :], share)
    before = jnp.where(
        lax.broadcasted_iota(jnp.int32, (tokens, tokens), 0)
        < lax.broadcasted_iota(jnp.int32, (tokens, tokens), 1),
        1.0,
        0.0,
    ).astype(BF16)
    rank = jnp.dot(named.astype(BF16), before, preferred_element_type=F32)
    chosen = jnp.logical_and(named > 0.5, rank == (slot % cap).astype(F32))
    pick_all = jnp.where(chosen, 1.0, 0.0).astype(BF16)
    mix = jnp.where(chosen, share, 0.0)
    mix_high = mix.astype(BF16)
    mixes[0] = mix_high
    mixes[1] = (mix - mix_high.astype(F32)).astype(BF16)

    own = jnp.zeros((tokens, 1), F32)
    for f in range(2):
        part_copy(f).wait_recv()
        at = pl.ds(f * wide, wide)
        state = resid[:, at].astype(F32) + (acc[f, :tokens, :] + part_in[f].astype(F32))
        hidden_buf[:, at] = state
        own += jnp.sum(state * state, axis=1, keepdims=True)
    squares[...] = jnp.broadcast_to(own, squares.shape)
    sq = pltpu.make_async_remote_copy(
        src_ref=squares, dst_ref=peer_squares, send_sem=sq_sem.at[0], recv_sem=sq_sem.at[1],
        device_id=(c, 1 - e), device_id_type=MESH,
    )
    sq.start()
    sq.wait()
    mean = (squares[:, :1] + peer_squares[:, :1]) / D
    normed = (hidden_buf[...] * lax.rsqrt(mean + epsilon) * gain_ref[...]).astype(BF16)
    normed_buf[...] = normed
    for j in range(blocks // 2):
        sent = jnp.dot(
            pick_all, normed_buf[:, j * 256 : (j + 1) * 256], preferred_element_type=F32
        )
        stage[pl.ds(2 * j, rows, stride=blocks), :] = sent[:, :128]
        stage[pl.ds(2 * j + 1, rows, stride=blocks), :] = sent[:, 128:]
    outbox[...] = stage[...].reshape(outbox.shape).astype(BF16)

    def a_copy(to):
        return pltpu.make_async_remote_copy(
            src_ref=outbox.at[to], dst_ref=inbox.at[c], send_sem=a_send.at[to],
            recv_sem=a_recv.at[c], device_id=(to, e), device_id_type=MESH,
        )

    def b_copy(to):
        return pltpu.make_async_remote_copy(
            src_ref=backbox.at[to], dst_ref=endbox.at[c], send_sem=b_send.at[to],
            recv_sem=b_recv.at[c], device_id=(to, e), device_id_type=MESH,
        )

    near_rows = rows // 2
    near_n = n // 2

    def half_of(t):
        return zh + t * (1 - 2 * zh)

    def from_half(box, sems, t):
        first = half_of(t) * near_n

        @pl.loop(0, near_n)
        def _(j):
            source = first + j

            @pl.when(source != c)
            def _():
                pltpu.make_async_remote_copy(
                    src_ref=box.at[source], dst_ref=box.at[source], send_sem=a_send.at[0],
                    recv_sem=sems.at[source], device_id=(source, e), device_id_type=MESH,
                ).wait_recv()

        part_stage = stage.at[pl.ds(0, near_rows * blocks)]
        part_stage[...] = box[pl.ds(first, near_n)].reshape(near_rows * blocks, 128).astype(F32)
        for j in range(blocks):
            two[t, :, j * 128 : (j + 1) * 128] = stage[
                pl.ds(j, near_rows, stride=blocks), :
            ].astype(BF16)

    def far_first(start):
        @pl.loop(0, near_n)
        def _(j):
            start((1 - zh) * near_n + (c + j) % near_n)

        @pl.loop(1, near_n)
        def _(j):
            start(zh * near_n + (c + j) % near_n)

    far_first(lambda to: a_copy(to).start())
    inbox[c] = outbox[c]
    unpack(3 * (n_unpack // 4), n_unpack // 4)
    width = parts.shape[4]

    def p_copy(t, m):
        return pltpu.make_async_remote_copy(
            src_ref=parts.at[t, m], dst_ref=peer_parts.at[t, m], send_sem=p_send.at[t, m],
            recv_sem=p_recv.at[t, m], device_id=(c, 1 - e), device_id_type=MESH,
        )

    n_parts = units // width

    @pl.loop(0, 2)
    def _(t):
        from_half(inbox, a_recv, t)
        for m in range(n_parts):
            for side in range(2):
                start = side * units + m * width
                parts[t, m, side] = jnp.dot(
                    two[t], gu[:, start : start + width], preferred_element_type=F32
                ).astype(BF16)
            p_copy(t, m).start()

    load_down.wait()

    @pl.loop(0, 2)
    def _(t):
        for m in range(n_parts):
            p_copy(t, m).wait_recv()
            gate = parts[t, m, 0].astype(F32) + peer_parts[t, m, 0].astype(F32)
            up = parts[t, m, 1].astype(F32) + peer_parts[t, m, 1].astype(F32)
            act[:, m * width : (m + 1) * width] = (gate / (1.0 + jnp.exp(-gate)) * up).astype(BF16)
        for j in range(blocks // 2):
            result = jnp.dot(
                act[...], down[:, j * 256 : (j + 1) * 256], preferred_element_type=F32
            )
            stage[pl.ds(2 * j, near_rows, stride=blocks), :] = result[:, :128]
            stage[pl.ds(2 * j + 1, near_rows, stride=blocks), :] = result[:, 128:]
        first = half_of(t) * near_n
        backbox[pl.ds(first, near_n)] = (
            stage[: near_rows * blocks, :].reshape((near_n,) + backbox.shape[1:]).astype(BF16)
        )

        @pl.loop(0, near_n)
        def _(j):
            to = first + (c + j) % near_n

            @pl.when(to != c)
            def _():
                b_copy(to).start()

    endbox[c] = backbox[c]

    @pl.loop(0, 2)
    def _(t):
        from_half(endbox, b_recv, t)
        at = pl.ds(pl.multiple_of(half_of(t) * near_rows, 16), near_rows)
        for part in range(2):
            hidden_buf[...] += lax.dot_general(
                mixes[part, at, :], two[t], (((0,), (0,)), ((), ())), preferred_element_type=F32
            )

    mixed_ref[...] = hidden_buf[...].astype(BF16)

    for slot_index in range(15):
        kv_copy(c, slot_index, sibling).wait_send()
    for f in range(2):
        swap(f).wait_send()
        part_copy(f).wait_send()
        to_partner(f).wait_send()
        over(0, f).wait_send()
        over(1, f).wait_send()

    @pl.loop(0, 2)
    def _(g):
        w_copy(mine, 0, g, fwd_y.at[g], sibling).wait_send()
        w_copy(mine, 0, g, fwd_z.at[g], sibling).wait_send()
        for f in range(2):
            w_copy(mine, f, g, own_z.at[f, g], sibling).wait_send()
            w_copy(mine, f, g, own_y.at[f, g], sibling).wait_send()
            for source in range(4):
                w_copy(mine, f, g, w_sib.at[source, f, g], sibling).wait_send()

    @pl.loop(1, n)
    def _(j):
        a_copy((c + j) % n).wait_send()
        b_copy((c + j) % n).wait_send()

    for t in range(2):
        for m in range(n_parts):
            p_copy(t, m).wait_send()


def fast_body(queries, keys, values, resid, gain, expert_ids, gate_scores, w_gate_up, w_down, w_out):
    tokens, heads, size = queries.shape
    n = lax.axis_size("ctx")
    half = resid.shape[1]
    wide = half // 2
    capacity = max(2, 5 * tokens * TOPK // (4 * EXPERTS))
    depth = heads * w_out.shape[1]
    units = w_down.shape[1]
    rows = n * capacity
    blocks = half // 128
    box = (n, capacity, blocks, 128)
    width = 256
    vmem = pl.BlockSpec(memory_space=pltpu.VMEM)
    hbm = pl.BlockSpec(memory_space=pltpu.HBM)
    dma = pltpu.SemaphoreType.DMA
    context, mixed = pl.pallas_call(
        layer_kernel,
        out_shape=(
            jax.ShapeDtypeStruct((tokens * heads, size), BF16),
            jax.ShapeDtypeStruct((tokens, half), BF16),
        ),
        in_specs=[hbm] * 10,
        out_specs=(vmem, vmem),
        scratch_shapes=[
            pltpu.VMEM(keys.shape, BF16), pltpu.VMEM(values.shape, BF16), pltpu.VMEM((1, half), F32),
            pltpu.VMEM((TOPK, tokens), jnp.int32), pltpu.VMEM((TOPK, tokens), F32),
            pltpu.VMEM((tokens * heads, size), BF16),
            pltpu.VMEM((tokens, half), BF16),
            pltpu.VMEM((n, 2 * tokens, size), BF16),
            pltpu.VMEM((2, HALF_Z, 2, depth, wide), BF16),
            pltpu.VMEM((tokens * heads, size), F32),
            pltpu.VMEM((2, tokens, heads * size // 2), BF16),
            pltpu.VMEM((3, 2, 2, HALF_Z // PLANE, tokens, PLANE * depth // 2), BF16),
            pltpu.VMEM((heads * size // 2, PLANE * depth // 2), jnp.int32),
            pltpu.VMEM((2, 2 * tokens, wide), F32),
            pltpu.VMEM((2, tokens, wide), BF16),
            pltpu.VMEM((2, tokens, wide), BF16),
            pltpu.VMEM((half, 2, units), BF16),
            pltpu.VMEM((half, 2 * units), BF16),
            pltpu.VMEM((units, half), BF16),
            pltpu.VMEM((tokens, 128), F32),
            pltpu.VMEM((tokens, 128), F32),
            pltpu.VMEM((tokens, half), F32),
            pltpu.VMEM((rows * blocks, 128), F32),
            pltpu.VMEM((2, rows // 2, half), BF16),
            pltpu.VMEM(box, BF16), pltpu.VMEM(box, BF16), pltpu.VMEM(box, BF16), pltpu.VMEM(box, BF16),
            pltpu.VMEM((2, units // width, 2, rows // 2, width), BF16),
            pltpu.VMEM((2, units // width, 2, rows // 2, width), BF16),
            pltpu.VMEM((rows // 2, units), BF16),
            pltpu.VMEM((2, rows, tokens), BF16),
            pltpu.VMEM((tokens, half), BF16),
            dma((15,)), dma((n,)), dma((2, 2)), dma((2,)), dma((2, 2)), dma((2,)),
            dma((4, 2, 2)), dma((HALF_Z, 2, 2)), dma((2,)), dma((3, 2)), dma((3, 2)), dma((2,)), dma((2,)),
            dma((2,)), dma((2, units // width)), dma((2, units // width)),
            dma((n,)), dma((n,)), dma((n,)), dma((n,)), dma((11,)),
        ],
        compiler_params=pltpu.CompilerParams(
            collective_id=0, has_side_effects=True, vmem_limit_bytes=56 * 2**20
        ),
        name="layer",
    )(
        queries.reshape(tokens * heads, size), keys, values,
        w_out.reshape(depth, 2 * half), resid, gain.reshape(1, half), expert_ids.T, gate_scores.T,
        w_gate_up[0], w_down[0],
    )
    return (context.reshape(tokens, heads, size), mixed)


def solution(mesh):
    in_specs = (
        P("ctx", "exp", None),
        P("ctx", None, None),
        P("ctx", None, None),
        P("ctx", "exp"),
        P("exp"),
        P("ctx", None),
        P("ctx", None),
        P("ctx", "exp", None, None),
        P("ctx", None, "exp"),
        P("exp", "ctx", None),
    )
    out_specs = (P("ctx", "exp", None), P("ctx", "exp"))
    fits = mesh.shape["ctx"] == N_Z * PLANE and mesh.shape["exp"] == 2
    body = fast_body if fits else general_body
    return jax.shard_map(body, mesh=mesh, in_specs=in_specs, out_specs=out_specs, check_vma=False)
```

```python
import functools
import math

import jax
import jax.numpy as jnp
from jax import lax
from jax.experimental import pallas as pl
from jax.experimental.pallas import tpu as pltpu
from jax.sharding import PartitionSpec as P

D = 4096
HQ = 32
KVH = 2
EXPERTS = 128
TOPK = 8


masked_score = -1e30
epsilon = 1e-06


def attend_piece(state_now, pair_piece, offset, query_rows, query_pos, last_pos, scaling):
    key_piece, value_piece = pair_piece
    length = key_piece.shape[0]

    def compute(state_in):
        running, denominator, numerator = state_in
        scores = (
            jnp.einsum("rd,kd->rk", query_rows, key_piece, preferred_element_type=jnp.float32)
            * scaling
        )
        key_pos = jnp.arange(length, dtype=jnp.int32)
        visible = key_pos[None, :] <= query_pos[:, None]
        masked = jnp.where(visible, scores, masked_score)
        highest = jnp.maximum(running, jnp.max(masked, axis=1))
        weights_exp = jnp.where(visible, jnp.exp(masked - highest[:, None]), 0.0)
        rounded = weights_exp.astype(jnp.bfloat16)
        numerator = jnp.dot(rounded, value_piece, preferred_element_type=jnp.float32)
        denominator = jnp.sum(weights_exp, axis=1)
        return (highest, denominator, numerator)

    def untouched(state_in):
        return state_in

    return lax.cond(offset <= last_pos, compute, untouched, state_now)


def general_body(queries, keys, values, resid, gain, expert_ids, gate_scores, w_gate_up, w_down, w_out):
    tokens_here = queries.shape[0]
    heads_here = queries.shape[1]
    head_size = queries.shape[2]
    ctx_count = lax.axis_size("ctx")
    ctx_place = lax.axis_index("ctx")
    exp_place = lax.axis_index("exp")
    own_pos = ctx_place * tokens_here + jnp.arange(tokens_here, dtype=jnp.int32)
    query_sets = (queries, own_pos)
    group_index = exp_place * heads_here // (HQ // KVH)
    key_local = lax.dynamic_index_in_dim(keys, group_index, 1, keepdims=False)
    value_local = lax.dynamic_index_in_dim(values, group_index, 1, keepdims=False)
    scaling = 1.0 / math.sqrt(head_size)
    set_queries, set_pos = query_sets
    set_rows = set_queries.shape[0] * heads_here
    initial = [
        (
            jnp.full((set_rows,), masked_score, jnp.float32),
            jnp.zeros((set_rows,), jnp.float32),
            jnp.zeros((set_rows, head_size), jnp.float32),
        )
    ]
    rows_set = set_queries.reshape(set_rows, head_size)
    pos_set = jnp.repeat(set_pos, heads_here)
    last_set = jnp.max(set_pos)
    updated = [
        attend_piece(
            tuple(initial)[0],
            (
                lax.all_gather(key_local, "ctx", axis=0, tiled=True),
                lax.all_gather(value_local, "ctx", axis=0, tiled=True),
            ),
            jnp.int32(0),
            rows_set,
            pos_set,
            last_set,
            scaling,
        )
    ]
    folded = tuple(updated)
    pieces_out = []
    for state_set in folded:
        normalized = state_set[2] / state_set[1][:, None]
        pieces_out.append(normalized.reshape(-1, heads_here, head_size).astype(jnp.bfloat16))
    context = pieces_out[0]
    whole_out = lax.all_gather(w_out, "ctx", axis=1, tiled=True)
    projected = jnp.einsum("thp,hpd->td", context, whole_out, preferred_element_type=jnp.float32)
    attended = lax.psum_scatter(
        projected.astype(jnp.bfloat16), "exp", scatter_dimension=1, tiled=True
    ).astype(jnp.float32)
    hidden_state = resid.astype(jnp.float32) + attended
    square_sum = lax.psum(jnp.sum(hidden_state * hidden_state, axis=1), "exp")
    inverse = lax.rsqrt(square_sum / D + epsilon)
    normed = (hidden_state * inverse[:, None] * gain[None, :]).astype(jnp.bfloat16)
    capacity = max(2, 5 * tokens_here * TOPK // (4 * EXPERTS))
    flat_ids = expert_ids.reshape(-1)
    onehot = (flat_ids[:, None] == jnp.arange(ctx_count, dtype=jnp.int32)[None, :]).astype(
        jnp.int32
    )
    earlier = jnp.cumsum(onehot, axis=0) - onehot
    rank_of = jnp.sum(earlier * onehot, axis=1)
    active = flat_ids < ctx_count
    slot_of = jnp.where(active, flat_ids * capacity + rank_of, -1).reshape(tokens_here, TOPK)
    slot_range = jnp.arange(ctx_count * capacity, dtype=jnp.int32)
    dispatch_map = jnp.zeros((ctx_count * capacity, tokens_here), jnp.bfloat16)
    for column in range(TOPK):
        dispatch_map = dispatch_map + (slot_range[:, None] == slot_of[None, :, column]).astype(
            jnp.bfloat16
        )
    local_width = normed.shape[1]
    outgoing = jnp.dot(dispatch_map, normed, preferred_element_type=jnp.float32).astype(
        jnp.bfloat16
    )
    outgoing = outgoing.reshape(ctx_count, capacity, local_width)
    arrived = lax.all_to_all(outgoing, "ctx", split_axis=0, concat_axis=0, tiled=True)
    sources = arrived.shape[0]
    width_slots = arrived.shape[1]
    row_block = arrived.reshape(sources * width_slots, local_width)
    partial_sum = jnp.einsum(
        "rd,dgf->rgf", row_block, w_gate_up[0], preferred_element_type=jnp.float32
    )
    summed = lax.psum(partial_sum.astype(jnp.bfloat16), "exp").astype(jnp.float32)
    hidden_units = (jax.nn.silu(summed[:, 0]) * summed[:, 1]).astype(jnp.bfloat16)
    result = jnp.dot(hidden_units, w_down[0], preferred_element_type=jnp.float32).astype(
        jnp.bfloat16
    )
    result = result.reshape(sources, width_slots, local_width)
    returned = lax.all_to_all(result, "ctx", split_axis=0, concat_axis=0, tiled=True)
    back_rows = returned.reshape(ctx_count * capacity, local_width)
    picked = jnp.take(back_rows, jnp.maximum(slot_of, 0).reshape(-1), axis=0).reshape(
        tokens_here, TOPK, local_width
    )
    weight_now = gate_scores / jnp.sum(gate_scores, axis=1, keepdims=True)
    weight_now = jnp.where(active.reshape(tokens_here, TOPK), weight_now, 0.0)
    routed = jnp.zeros((tokens_here, local_width), jnp.float32)
    for column in range(TOPK):
        routed = routed + weight_now[:, column : column + 1] * picked[:, column].astype(jnp.float32)
    mixed = (hidden_state + routed).astype(jnp.bfloat16)
    return (context, mixed)


MESH = pl.DeviceIdType.MESH
F32 = jnp.float32
BF16 = jnp.bfloat16
N_Z = 4
PLANE = 4
HALF_Z = 8


def layer_kernel(
    q_hbm, key_hbm, value_hbm, w_hbm, resid_hbm, gain_hbm, ids_hbm, gate_hbm, gu_hbm, down_hbm,
    ctx_ref, mixed_ref,
    key_ref, value_ref, gain_ref, ids_ref, gate_ref, q_in, resid, kvbuf, wbuf, rows32, ctx2d, ctxbuf, target, acc, part_out, part_in,
    gu, down, squares, peer_squares, hidden_buf, stage, two, outbox, inbox, backbox, endbox,
    parts, peer_parts, act, mixes, normed_buf,
    kv_send, kv_recv, own_z, fwd_z, own_y, fwd_y, w_sib, w_recv, x_send, c_send, c_recv, h_send, h_recv,
    sq_sem, p_send, p_recv, a_send, a_recv, b_send, b_recv, local_sem,
):
    c = lax.axis_index("ctx")
    e = lax.axis_index("exp")
    n = inbox.shape[0]
    cap = inbox.shape[1]
    rows = n * cap
    blocks = inbox.shape[2]
    z = c // PLANE
    zh = z // 2
    zl = z % 2
    y = (c // 2) % 2
    k = c % 2
    plane = c % PLANE
    z_peer = c + PLANE * (1 - 2 * zl)
    y_peer = c + 2 * (1 - 2 * y)
    sibling = c + 1 - 2 * k
    partner = c + HALF_Z * (1 - 2 * zh)
    half = resid.shape[1]
    tokens = resid.shape[0]
    heads = q_in.shape[0] // tokens
    wide = wbuf.shape[4]
    depth = wbuf.shape[3]

    def block_of(other_z, other_y, other_k):
        in_z = zl + other_z * (1 - 2 * zl)
        in_y = y + other_y * (1 - 2 * y)
        in_k = k + other_k * (1 - 2 * k)
        return in_z * PLANE + in_y * 2 + in_k

    barrier = pltpu.get_barrier_semaphore()

    @pl.loop(1, n)
    def _(j):
        pl.semaphore_signal(barrier, inc=1, device_id=((c + j) % n, e), device_id_type=MESH)

    pl.semaphore_signal(barrier, inc=1, device_id=(c, 1 - e), device_id_type=MESH)
    mine = block_of(0, 0, 0)

    def own_load(f):
        return pltpu.make_async_copy(
            w_hbm.at[:, pl.ds(pl.multiple_of(e * half + f * wide, wide), wide)],
            wbuf.at[f, mine, e], local_sem.at[f],
        )

    load_q = pltpu.make_async_copy(q_hbm, q_in, local_sem.at[2])
    load_resid = pltpu.make_async_copy(resid_hbm, resid, local_sem.at[3])
    load_gu = pltpu.make_async_copy(gu_hbm, gu, local_sem.at[4])
    load_down = pltpu.make_async_copy(down_hbm, down, local_sem.at[5])
    small = [
        pltpu.make_async_copy(source, held, local_sem.at[6 + i])
        for i, (source, held) in enumerate(
            (
                (key_hbm, key_ref), (value_hbm, value_ref), (gain_hbm, gain_ref),
                (ids_hbm, ids_ref), (gate_hbm, gate_ref),
            )
        )
    ]
    for copy in small:
        copy.start()
    own_load(0).start()
    own_load(1).start()
    load_q.start()
    load_resid.start()
    load_gu.start()
    load_down.start()
    small[0].wait()
    small[1].wait()
    group = e * heads // (HQ // KVH)
    for part, source in enumerate((key_ref, value_ref)):
        picked = jnp.where(group == 0, source[:, 0, :].astype(F32), source[:, 1, :].astype(F32))
        kvbuf[c, part * tokens : (part + 1) * tokens, :] = picked.astype(BF16)
    pl.semaphore_wait(barrier, n)

    def kv_copy(block, slot, to):
        return pltpu.make_async_remote_copy(
            src_ref=kvbuf.at[block], dst_ref=kvbuf.at[block], send_sem=kv_send.at[slot],
            recv_sem=kv_recv.at[block], device_id=(to, e), device_id_type=MESH,
        )

    def w_copy(block, f, g, sem, to):
        return pltpu.make_async_remote_copy(
            src_ref=wbuf.at[f, block, g], dst_ref=wbuf.at[f, block, g], send_sem=sem,
            recv_sem=w_recv.at[block, f, g], device_id=(to, e), device_id_type=MESH,
        )

    def wait_block(block, f, g):
        w_copy(block, f, g, own_z.at[0, 0], sibling).wait_recv()

    def swap(f):
        return pltpu.make_async_remote_copy(
            src_ref=w_hbm.at[:, pl.ds(pl.multiple_of((1 - e) * half + f * wide, wide), wide)],
            dst_ref=wbuf.at[f, mine, e], send_sem=x_send.at[f], recv_sem=w_recv.at[mine, f, e],
            device_id=(c, 1 - e), device_id_type=MESH,
        )

    def group_of(s):
        return (e + s) % 2

    def send_own(f, s):
        g = group_of(s)
        w_copy(mine, f, g, own_z.at[f, g], z_peer).start()
        w_copy(mine, f, g, own_y.at[f, g], y_peer).start()
        w_copy(mine, f, g, w_sib.at[0, f, g], sibling).start()

    for step in range(1, N_Z):
        kv_copy(c, step - 1, ((z + step) % N_Z) * PLANE + plane).start()
    kv_copy(c, 3, y_peer).start()
    kv_copy(c, 7, sibling).start()
    swap(0).start()
    swap(1).start()
    load_q.wait()
    rows32[...] = q_in[...].astype(F32)
    for step in range(1, N_Z):
        block = ((z + step) % N_Z) * PLANE + plane
        kv_copy(block, 0, sibling).wait_recv()
        kv_copy(block, 3 + step, y_peer).start()
        kv_copy(block, 7 + step, sibling).start()
    own_load(0).wait()
    send_own(0, 0)
    wait_block(mine, 0, group_of(1))
    send_own(0, 1)
    own_load(1).wait()
    send_own(1, 0)
    wait_block(mine, 1, group_of(1))
    send_own(1, 1)
    for step in range(N_Z):
        block = ((z + step) % N_Z) * PLANE + (1 - y) * 2 + k
        kv_copy(block, 0, sibling).wait_recv()
        kv_copy(block, 11 + step, sibling).start()
    depth_part = depth // 2
    row = lax.broadcasted_iota(jnp.int32, target.shape, 0)
    col = lax.broadcasted_iota(jnp.int32, target.shape, 1)
    target[...] = row - ((col % depth_part) // 8) * 128 - (col // depth_part) * 8 - col % 8
    for block_z in range(N_Z):
        for block_y in range(2):
            kv_copy(block_z * PLANE + block_y * 2 + 1 - k, 0, sibling).wait_recv()

    scale = math.log2(math.e) / math.sqrt(q_in.shape[1])
    n_keys = n * tokens

    def attend(pair):
        first = rows32[pl.ds(2 * pair, tokens, stride=heads), :]
        second = rows32[pl.ds(2 * pair + 1, tokens, stride=heads), :]
        both = jnp.concatenate([first, second], axis=0).astype(BF16)
        key_all = kvbuf[:, :tokens, :].reshape(n_keys, 128)
        value_all = kvbuf[:, tokens:, :].reshape(n_keys, 128)
        scores = lax.dot_general(
            both, key_all, (((1,), (1,)), ((), ())), preferred_element_type=F32
        )
        q_pos = c * tokens + lax.broadcasted_iota(jnp.int32, scores.shape, 0) % tokens
        k_pos = lax.broadcasted_iota(jnp.int32, scores.shape, 1)
        masked = jnp.where(k_pos <= q_pos, scores, masked_score)
        best = jnp.max(masked, axis=1, keepdims=True)
        prob = jnp.exp2((masked - best) * scale)
        total = jnp.sum(prob, axis=1, keepdims=True)
        part = jnp.dot(prob.astype(BF16), value_all, preferred_element_type=F32)
        done = (part / total).astype(BF16)
        turn = pair // (heads // 4)
        at = pair % (heads // 4) * 256
        ctx2d[turn, :, pl.ds(pl.multiple_of(at, 256), 128)] = done[:tokens]
        ctx2d[turn, :, pl.ds(pl.multiple_of(at + 128, 128), 128)] = done[tokens:]
        rows32[pl.ds(2 * pair, tokens, stride=heads), :] = done[:tokens].astype(F32)
        rows32[pl.ds(2 * pair + 1, tokens, stride=heads), :] = done[tokens:].astype(F32)

    def ctx_copy(slot, hh, src, dst, to):
        return pltpu.make_async_remote_copy(
            src_ref=src, dst_ref=dst, send_sem=c_send.at[slot, hh], recv_sem=c_recv.at[slot, hh],
            device_id=to, device_id_type=MESH,
        )

    def to_partner(hh):
        return ctx_copy(0, hh, ctxbuf.at[2, 0, hh], ctxbuf.at[1, e, hh], (partner, e))

    def over(slot, hh):
        return ctx_copy(1 + slot, hh, ctxbuf.at[slot, e, hh], ctxbuf.at[slot, e, hh], (c, 1 - e))

    def pass_on(hh):
        ctx_copy(0, hh, ctxbuf.at[1, e, hh], ctxbuf.at[1, e, hh], (partner, e)).wait_recv()
        over(1, hh).start()

    def pick_quad(hh, quad):
        pick = jnp.where(target[...] == 32 * quad, 1.0, 0.0).astype(BF16)
        return jnp.dot(ctx2d[hh], pick, preferred_element_type=F32).astype(BF16)

    @pl.loop(0, 2)
    def _(turn):
        @pl.loop(0, heads // 4)
        def _(step):
            attend(turn * (heads // 4) + step)

        @pl.loop(0, 2)
        def _(quad):
            ctxbuf[2, 0, turn, quad] = pick_quad(turn, (1 - zh) * 2 + quad)

        to_partner(turn).start()

        @pl.loop(0, 2)
        def _(quad):
            ctxbuf[0, e, turn, quad] = pick_quad(turn, zh * 2 + quad)

        over(0, turn).start()

        @pl.when(turn == 0)
        def _():
            @pl.loop(0, 2)
            def _(s):
                g = group_of(s)
                wait_block(block_of(1, 0, 0), 0, g)
                w_copy(block_of(1, 0, 0), 0, g, fwd_y.at[g], y_peer).start()
                w_copy(block_of(1, 0, 0), 0, g, w_sib.at[1, 0, g], sibling).start()
                wait_block(block_of(0, 1, 0), 0, g)
                w_copy(block_of(0, 1, 0), 0, g, w_sib.at[2, 0, g], sibling).start()

    pass_on(0)

    @pl.loop(0, 2)
    def _(s):
        g = group_of(s)
        wait_block(block_of(0, 1, 0), 1, g)
        w_copy(block_of(0, 1, 0), 1, g, fwd_z.at[g], z_peer).start()
        w_copy(block_of(0, 1, 0), 1, g, w_sib.at[2, 1, g], sibling).start()
        wait_block(block_of(1, 0, 0), 1, g)
        w_copy(block_of(1, 0, 0), 1, g, w_sib.at[1, 1, g], sibling).start()

    units = down.shape[0]
    pass_on(1)

    def relay_far(f):
        @pl.loop(0, 2)
        def _(s):
            g = group_of(s)
            wait_block(block_of(1, 1, 0), f, g)
            w_copy(block_of(1, 1, 0), f, g, w_sib.at[3, f, g], sibling).start()

    relay_far(0)
    ctx_ref[...] = rows32[...].astype(BF16)
    acc[...] = jnp.zeros_like(acc)
    for hh in range(2):
        for slot in range(2):
            ctx_copy(
                1 + slot, hh, ctxbuf.at[slot, 1 - e, hh], ctxbuf.at[slot, 1 - e, hh], (c, 1 - e)
            ).wait_recv()

    def project(f):
        @pl.loop(0, 4)
        def _(i):
            other_z = i // 2
            g = group_of(i % 2)
            wait_block(block_of(other_z, 0, 1), f, g)
            wait_block(block_of(other_z, 1, 1), f, g)
            quad = zl + other_z * (1 - 2 * zl)
            for hh in range(2):
                weights = wbuf[
                    f, pl.ds(quad * PLANE, PLANE), pl.ds(g, 1), hh * depth_part : (hh + 1) * depth_part
                ].reshape(PLANE * depth_part, wide)
                lhs = jnp.concatenate([ctxbuf[0, g, hh, quad], ctxbuf[1, g, hh, quad]], axis=0)
                acc[f] += jnp.dot(lhs, weights, preferred_element_type=F32)

        part_out[f] = acc[f, tokens:, :].astype(BF16)
        pltpu.make_async_remote_copy(
            src_ref=part_out.at[f], dst_ref=part_in.at[f], send_sem=h_send.at[f],
            recv_sem=h_recv.at[f], device_id=(partner, e), device_id_type=MESH,
        ).start()

    def part_copy(f):
        return pltpu.make_async_remote_copy(
            src_ref=part_out.at[f], dst_ref=part_in.at[f], send_sem=h_send.at[f],
            recv_sem=h_recv.at[f], device_id=(partner, e), device_id_type=MESH,
        )

    project(0)
    relay_far(1)
    project(1)
    load_resid.wait()
    load_gu.wait()

    for copy in small[2:]:
        copy.wait()
    slot = lax.broadcasted_iota(jnp.int32, (rows, tokens), 0)
    named = jnp.zeros((rows, tokens), F32)
    share = jnp.zeros((rows, tokens), F32)
    gates = gate_ref[...]
    gates = gates / jnp.sum(gates, axis=0, keepdims=True)
    for column in range(TOPK):
        hit = ids_ref[column : column + 1, :] == slot // cap
        named = jnp.where(hit, 1.0, named)
        share = jnp.where(hit, gates[column : column + 1, :], share)
    before = jnp.where(
        lax.broadcasted_iota(jnp.int32, (tokens, tokens), 0)
        < lax.broadcasted_iota(jnp.int32, (tokens, tokens), 1),
        1.0,
        0.0,
    ).astype(BF16)
    rank = jnp.dot(named.astype(BF16), before, preferred_element_type=F32)
    chosen = jnp.logical_and(named > 0.5, rank == (slot % cap).astype(F32))
    pick_all = jnp.where(chosen, 1.0, 0.0).astype(BF16)
    mix = jnp.where(chosen, share, 0.0)
    mix_high = mix.astype(BF16)
    mixes[0] = mix_high
    mixes[1] = (mix - mix_high.astype(F32)).astype(BF16)

    own = jnp.zeros((tokens, 1), F32)
    for f in range(2):
        part_copy(f).wait_recv()
        at = pl.ds(f * wide, wide)
        state = resid[:, at].astype(F32) + (acc[f, :tokens, :] + part_in[f].astype(F32))
        hidden_buf[:, at] = state
        own += jnp.sum(state * state, axis=1, keepdims=True)
    squares[...] = jnp.broadcast_to(own, squares.shape)
    sq = pltpu.make_async_remote_copy(
        src_ref=squares, dst_ref=peer_squares, send_sem=sq_sem.at[0], recv_sem=sq_sem.at[1],
        device_id=(c, 1 - e), device_id_type=MESH,
    )
    sq.start()
    sq.wait()
    mean = (squares[:, :1] + peer_squares[:, :1]) / D
    normed = (hidden_buf[...] * lax.rsqrt(mean + epsilon) * gain_ref[...]).astype(BF16)
    normed_buf[...] = normed
    for j in range(blocks // 2):
        sent = jnp.dot(
            pick_all, normed_buf[:, j * 256 : (j + 1) * 256], preferred_element_type=F32
        )
        stage[pl.ds(2 * j, rows, stride=blocks), :] = sent[:, :128]
        stage[pl.ds(2 * j + 1, rows, stride=blocks), :] = sent[:, 128:]
    outbox[...] = stage[...].reshape(outbox.shape).astype(BF16)

    def a_copy(to):
        return pltpu.make_async_remote_copy(
            src_ref=outbox.at[to], dst_ref=inbox.at[c], send_sem=a_send.at[to],
            recv_sem=a_recv.at[c], device_id=(to, e), device_id_type=MESH,
        )

    def b_copy(to):
        return pltpu.make_async_remote_copy(
            src_ref=backbox.at[to], dst_ref=endbox.at[c], send_sem=b_send.at[to],
            recv_sem=b_recv.at[c], device_id=(to, e), device_id_type=MESH,
        )

    near_rows = rows // 2
    near_n = n // 2

    def half_of(t):
        return zh + t * (1 - 2 * zh)

    def from_half(box, sems, t):
        first = half_of(t) * near_n

        @pl.loop(0, near_n)
        def _(j):
            source = first + j

            @pl.when(source != c)
            def _():
                pltpu.make_async_remote_copy(
                    src_ref=box.at[source], dst_ref=box.at[source], send_sem=a_send.at[0],
                    recv_sem=sems.at[source], device_id=(source, e), device_id_type=MESH,
                ).wait_recv()

        part_stage = stage.at[pl.ds(0, near_rows * blocks)]
        part_stage[...] = box[pl.ds(first, near_n)].reshape(near_rows * blocks, 128).astype(F32)
        for j in range(blocks):
            two[t, :, j * 128 : (j + 1) * 128] = stage[
                pl.ds(j, near_rows, stride=blocks), :
            ].astype(BF16)

    def far_first(start):
        @pl.loop(0, near_n)
        def _(j):
            start((1 - zh) * near_n + (c + j) % near_n)

        @pl.loop(1, near_n)
        def _(j):
            start(zh * near_n + (c + j) % near_n)

    far_first(lambda to: a_copy(to).start())
    inbox[c] = outbox[c]
    width = parts.shape[4]

    def p_copy(t, m):
        return pltpu.make_async_remote_copy(
            src_ref=parts.at[t, m], dst_ref=peer_parts.at[t, m], send_sem=p_send.at[t, m],
            recv_sem=p_recv.at[t, m], device_id=(c, 1 - e), device_id_type=MESH,
        )

    n_parts = units // width

    @pl.loop(0, 2)
    def _(t):
        from_half(inbox, a_recv, t)
        for m in range(n_parts):
            for side in range(2):
                start = side * units + m * width
                parts[t, m, side] = jnp.dot(
                    two[t], gu[:, start : start + width], preferred_element_type=F32
                ).astype(BF16)
            p_copy(t, m).start()

    load_down.wait()

    @pl.loop(0, 2)
    def _(t):
        for m in range(n_parts):
            p_copy(t, m).wait_recv()
            gate = parts[t, m, 0].astype(F32) + peer_parts[t, m, 0].astype(F32)
            up = parts[t, m, 1].astype(F32) + peer_parts[t, m, 1].astype(F32)
            act[:, m * width : (m + 1) * width] = (gate / (1.0 + jnp.exp(-gate)) * up).astype(BF16)
        for j in range(blocks // 2):
            result = jnp.dot(
                act[...], down[:, j * 256 : (j + 1) * 256], preferred_element_type=F32
            )
            stage[pl.ds(2 * j, near_rows, stride=blocks), :] = result[:, :128]
            stage[pl.ds(2 * j + 1, near_rows, stride=blocks), :] = result[:, 128:]
        first = half_of(t) * near_n
        backbox[pl.ds(first, near_n)] = (
            stage[: near_rows * blocks, :].reshape((near_n,) + backbox.shape[1:]).astype(BF16)
        )

        @pl.loop(0, near_n)
        def _(j):
            to = first + (c + j) % near_n

            @pl.when(to != c)
            def _():
                b_copy(to).start()

    endbox[c] = backbox[c]

    @pl.loop(0, 2)
    def _(t):
        from_half(endbox, b_recv, t)
        at = pl.ds(pl.multiple_of(half_of(t) * near_rows, 16), near_rows)
        for part in range(2):
            hidden_buf[...] += lax.dot_general(
                mixes[part, at, :], two[t], (((0,), (0,)), ((), ())), preferred_element_type=F32
            )

    mixed_ref[...] = hidden_buf[...].astype(BF16)

    for slot_index in range(15):
        kv_copy(c, slot_index, sibling).wait_send()
    for f in range(2):
        swap(f).wait_send()
        part_copy(f).wait_send()
        to_partner(f).wait_send()
        over(0, f).wait_send()
        over(1, f).wait_send()

    @pl.loop(0, 2)
    def _(g):
        w_copy(mine, 0, g, fwd_y.at[g], sibling).wait_send()
        w_copy(mine, 0, g, fwd_z.at[g], sibling).wait_send()
        for f in range(2):
            w_copy(mine, f, g, own_z.at[f, g], sibling).wait_send()
            w_copy(mine, f, g, own_y.at[f, g], sibling).wait_send()
            for source in range(4):
                w_copy(mine, f, g, w_sib.at[source, f, g], sibling).wait_send()

    @pl.loop(1, n)
    def _(j):
        a_copy((c + j) % n).wait_send()
        b_copy((c + j) % n).wait_send()

    for t in range(2):
        for m in range(n_parts):
            p_copy(t, m).wait_send()


def hand_over(context_in, mixed_in, context_out, mixed_out, sem):
    first = pltpu.make_async_copy(context_in, context_out, sem.at[0])
    second = pltpu.make_async_copy(mixed_in, mixed_out, sem.at[1])
    first.start()
    second.start()
    first.wait()
    second.wait()


def fast_body(queries, keys, values, resid, gain, expert_ids, gate_scores, w_gate_up, w_down, w_out):
    tokens, heads, size = queries.shape
    n = lax.axis_size("ctx")
    half = resid.shape[1]
    wide = half // 2
    capacity = max(2, 5 * tokens * TOPK // (4 * EXPERTS))
    depth = heads * w_out.shape[1]
    units = w_down.shape[1]
    rows = n * capacity
    blocks = half // 128
    box = (n, capacity, blocks, 128)
    width = 256
    vmem = pl.BlockSpec(memory_space=pltpu.VMEM)
    hbm = pl.BlockSpec(memory_space=pltpu.HBM)
    dma = pltpu.SemaphoreType.DMA
    context, mixed = pl.pallas_call(
        layer_kernel,
        out_shape=(
            jax.ShapeDtypeStruct((tokens * heads, size), BF16),
            jax.ShapeDtypeStruct((tokens, half), BF16),
        ),
        in_specs=[hbm] * 10,
        out_specs=(vmem, vmem),
        scratch_shapes=[
            pltpu.VMEM(keys.shape, BF16), pltpu.VMEM(values.shape, BF16), pltpu.VMEM((1, half), F32),
            pltpu.VMEM((TOPK, tokens), jnp.int32), pltpu.VMEM((TOPK, tokens), F32),
            pltpu.VMEM((tokens * heads, size), BF16),
            pltpu.VMEM((tokens, half), BF16),
            pltpu.VMEM((n, 2 * tokens, size), BF16),
            pltpu.VMEM((2, HALF_Z, 2, depth, wide), BF16),
            pltpu.VMEM((tokens * heads, size), F32),
            pltpu.VMEM((2, tokens, heads * size // 2), BF16),
            pltpu.VMEM((3, 2, 2, HALF_Z // PLANE, tokens, PLANE * depth // 2), BF16),
            pltpu.VMEM((heads * size // 2, PLANE * depth // 2), jnp.int32),
            pltpu.VMEM((2, 2 * tokens, wide), F32),
            pltpu.VMEM((2, tokens, wide), BF16),
            pltpu.VMEM((2, tokens, wide), BF16),
            pltpu.VMEM((half, 2 * units), BF16),
            pltpu.VMEM((units, half), BF16),
            pltpu.VMEM((tokens, 128), F32),
            pltpu.VMEM((tokens, 128), F32),
            pltpu.VMEM((tokens, half), F32),
            pltpu.VMEM((rows * blocks, 128), F32),
            pltpu.VMEM((2, rows // 2, half), BF16),
            pltpu.VMEM(box, BF16), pltpu.VMEM(box, BF16), pltpu.VMEM(box, BF16), pltpu.VMEM(box, BF16),
            pltpu.VMEM((2, units // width, 2, rows // 2, width), BF16),
            pltpu.VMEM((2, units // width, 2, rows // 2, width), BF16),
            pltpu.VMEM((rows // 2, units), BF16),
            pltpu.VMEM((2, rows, tokens), BF16),
            pltpu.VMEM((tokens, half), BF16),
            dma((15,)), dma((n,)), dma((2, 2)), dma((2,)), dma((2, 2)), dma((2,)),
            dma((4, 2, 2)), dma((HALF_Z, 2, 2)), dma((2,)), dma((3, 2)), dma((3, 2)), dma((2,)), dma((2,)),
            dma((2,)), dma((2, units // width)), dma((2, units // width)),
            dma((n,)), dma((n,)), dma((n,)), dma((n,)), dma((11,)),
        ],
        compiler_params=pltpu.CompilerParams(
            collective_id=0, has_side_effects=True, vmem_limit_bytes=56 * 2**20
        ),
        name="layer",
    )(
        queries.reshape(tokens * heads, size), keys, values,
        w_out.reshape(depth, 2 * half), resid, gain.reshape(1, half), expert_ids.T, gate_scores.T,
        w_gate_up[0].reshape(half, 2 * units), w_down[0],
    )
    context, mixed = pl.pallas_call(
        hand_over,
        out_shape=(
            jax.ShapeDtypeStruct((tokens * heads, size), BF16),
            jax.ShapeDtypeStruct((tokens, half), BF16),
        ),
        in_specs=[hbm, hbm],
        out_specs=(hbm, hbm),
        scratch_shapes=[dma((2,))],
        compiler_params=pltpu.CompilerParams(vmem_limit_bytes=56 * 2**20),
        name="hand_over",
    )(context, mixed)
    return (context.reshape(tokens, heads, size), mixed)


def solution(mesh):
    in_specs = (
        P("ctx", "exp", None),
        P("ctx", None, None),
        P("ctx", None, None),
        P("ctx", "exp"),
        P("exp"),
        P("ctx", None),
        P("ctx", None),
        P("ctx", "exp", None, None),
        P("ctx", None, "exp"),
        P("exp", "ctx", None),
    )
    out_specs = (P("ctx", "exp", None), P("ctx", "exp"))
    fits = mesh.shape["ctx"] == N_Z * PLANE and mesh.shape["exp"] == 2
    body = fast_body if fits else general_body
    return jax.shard_map(body, mesh=mesh, in_specs=in_specs, out_specs=out_specs, check_vma=False)
```

```python
import functools
import math

import jax
import jax.numpy as jnp
from jax import lax
from jax.experimental import pallas as pl
from jax.experimental.pallas import tpu as pltpu
from jax.sharding import PartitionSpec as P

D = 4096
HQ = 32
KVH = 2
EXPERTS = 128
TOPK = 8


masked_score = -1e30
epsilon = 1e-06


def attend_piece(state_now, pair_piece, offset, query_rows, query_pos, last_pos, scaling):
    key_piece, value_piece = pair_piece
    length = key_piece.shape[0]

    def compute(state_in):
        running, denominator, numerator = state_in
        scores = (
            jnp.einsum("rd,kd->rk", query_rows, key_piece, preferred_element_type=jnp.float32)
            * scaling
        )
        key_pos = jnp.arange(length, dtype=jnp.int32)
        visible = key_pos[None, :] <= query_pos[:, None]
        masked = jnp.where(visible, scores, masked_score)
        highest = jnp.maximum(running, jnp.max(masked, axis=1))
        weights_exp = jnp.where(visible, jnp.exp(masked - highest[:, None]), 0.0)
        rounded = weights_exp.astype(jnp.bfloat16)
        numerator = jnp.dot(rounded, value_piece, preferred_element_type=jnp.float32)
        denominator = jnp.sum(weights_exp, axis=1)
        return (highest, denominator, numerator)

    def untouched(state_in):
        return state_in

    return lax.cond(offset <= last_pos, compute, untouched, state_now)


def general_body(queries, keys, values, resid, gain, expert_ids, gate_scores, w_gate_up, w_down, w_out):
    tokens_here = queries.shape[0]
    heads_here = queries.shape[1]
    head_size = queries.shape[2]
    ctx_count = lax.axis_size("ctx")
    ctx_place = lax.axis_index("ctx")
    exp_place = lax.axis_index("exp")
    own_pos = ctx_place * tokens_here + jnp.arange(tokens_here, dtype=jnp.int32)
    query_sets = (queries, own_pos)
    group_index = exp_place * heads_here // (HQ // KVH)
    key_local = lax.dynamic_index_in_dim(keys, group_index, 1, keepdims=False)
    value_local = lax.dynamic_index_in_dim(values, group_index, 1, keepdims=False)
    scaling = 1.0 / math.sqrt(head_size)
    set_queries, set_pos = query_sets
    set_rows = set_queries.shape[0] * heads_here
    initial = [
        (
            jnp.full((set_rows,), masked_score, jnp.float32),
            jnp.zeros((set_rows,), jnp.float32),
            jnp.zeros((set_rows, head_size), jnp.float32),
        )
    ]
    rows_set = set_queries.reshape(set_rows, head_size)
    pos_set = jnp.repeat(set_pos, heads_here)
    last_set = jnp.max(set_pos)
    updated = [
        attend_piece(
            tuple(initial)[0],
            (
                lax.all_gather(key_local, "ctx", axis=0, tiled=True),
                lax.all_gather(value_local, "ctx", axis=0, tiled=True),
            ),
            jnp.int32(0),
            rows_set,
            pos_set,
            last_set,
            scaling,
        )
    ]
    folded = tuple(updated)
    pieces_out = []
    for state_set in folded:
        normalized = state_set[2] / state_set[1][:, None]
        pieces_out.append(normalized.reshape(-1, heads_here, head_size).astype(jnp.bfloat16))
    context = pieces_out[0]
    whole_out = lax.all_gather(w_out, "ctx", axis=1, tiled=True)
    projected = jnp.einsum("thp,hpd->td", context, whole_out, preferred_element_type=jnp.float32)
    attended = lax.psum_scatter(
        projected.astype(jnp.bfloat16), "exp", scatter_dimension=1, tiled=True
    ).astype(jnp.float32)
    hidden_state = resid.astype(jnp.float32) + attended
    square_sum = lax.psum(jnp.sum(hidden_state * hidden_state, axis=1), "exp")
    inverse = lax.rsqrt(square_sum / D + epsilon)
    normed = (hidden_state * inverse[:, None] * gain[None, :]).astype(jnp.bfloat16)
    capacity = max(2, 5 * tokens_here * TOPK // (4 * EXPERTS))
    flat_ids = expert_ids.reshape(-1)
    onehot = (flat_ids[:, None] == jnp.arange(ctx_count, dtype=jnp.int32)[None, :]).astype(
        jnp.int32
    )
    earlier = jnp.cumsum(onehot, axis=0) - onehot
    rank_of = jnp.sum(earlier * onehot, axis=1)
    active = flat_ids < ctx_count
    slot_of = jnp.where(active, flat_ids * capacity + rank_of, -1).reshape(tokens_here, TOPK)
    slot_range = jnp.arange(ctx_count * capacity, dtype=jnp.int32)
    dispatch_map = jnp.zeros((ctx_count * capacity, tokens_here), jnp.bfloat16)
    for column in range(TOPK):
        dispatch_map = dispatch_map + (slot_range[:, None] == slot_of[None, :, column]).astype(
            jnp.bfloat16
        )
    local_width = normed.shape[1]
    outgoing = jnp.dot(dispatch_map, normed, preferred_element_type=jnp.float32).astype(
        jnp.bfloat16
    )
    outgoing = outgoing.reshape(ctx_count, capacity, local_width)
    arrived = lax.all_to_all(outgoing, "ctx", split_axis=0, concat_axis=0, tiled=True)
    sources = arrived.shape[0]
    width_slots = arrived.shape[1]
    row_block = arrived.reshape(sources * width_slots, local_width)
    partial_sum = jnp.einsum(
        "rd,dgf->rgf", row_block, w_gate_up[0], preferred_element_type=jnp.float32
    )
    summed = lax.psum(partial_sum.astype(jnp.bfloat16), "exp").astype(jnp.float32)
    hidden_units = (jax.nn.silu(summed[:, 0]) * summed[:, 1]).astype(jnp.bfloat16)
    result = jnp.dot(hidden_units, w_down[0], preferred_element_type=jnp.float32).astype(
        jnp.bfloat16
    )
    result = result.reshape(sources, width_slots, local_width)
    returned = lax.all_to_all(result, "ctx", split_axis=0, concat_axis=0, tiled=True)
    back_rows = returned.reshape(ctx_count * capacity, local_width)
    picked = jnp.take(back_rows, jnp.maximum(slot_of, 0).reshape(-1), axis=0).reshape(
        tokens_here, TOPK, local_width
    )
    weight_now = gate_scores / jnp.sum(gate_scores, axis=1, keepdims=True)
    weight_now = jnp.where(active.reshape(tokens_here, TOPK), weight_now, 0.0)
    routed = jnp.zeros((tokens_here, local_width), jnp.float32)
    for column in range(TOPK):
        routed = routed + weight_now[:, column : column + 1] * picked[:, column].astype(jnp.float32)
    mixed = (hidden_state + routed).astype(jnp.bfloat16)
    return (context, mixed)


MESH = pl.DeviceIdType.MESH
F32 = jnp.float32
BF16 = jnp.bfloat16
N_Z = 4
PLANE = 4
HALF_Z = 8


def layer_kernel(
    q_hbm, key_hbm, value_hbm, w_hbm, resid_hbm, gain_hbm, ids_hbm, gate_hbm, gu_hbm, down_hbm,
    ctx_ref, mixed_ref,
    key_ref, value_ref, gain_ref, ids_ref, gate_ref, w_held, q_in, resid, kvbuf, wbuf, rows32, ctx2d, ctxbuf, target, acc, part_out, part_in,
    gu_raw, gu, down, squares, peer_squares, hidden_buf, stage, two, outbox, inbox, backbox, endbox,
    parts, peer_parts, act, mixes, normed_buf,
    kv_send, kv_recv, own_z, fwd_z, own_y, fwd_y, w_sib, w_recv, x_send, c_send, c_recv, h_send, h_recv,
    sq_sem, p_send, p_recv, a_send, a_recv, b_send, b_recv, local_sem,
):
    c = lax.axis_index("ctx")
    e = lax.axis_index("exp")
    n = inbox.shape[0]
    cap = inbox.shape[1]
    rows = n * cap
    blocks = inbox.shape[2]
    z = c // PLANE
    zh = z // 2
    zl = z % 2
    y = (c // 2) % 2
    k = c % 2
    plane = c % PLANE
    z_peer = c + PLANE * (1 - 2 * zl)
    y_peer = c + 2 * (1 - 2 * y)
    sibling = c + 1 - 2 * k
    partner = c + HALF_Z * (1 - 2 * zh)
    half = resid.shape[1]
    tokens = resid.shape[0]
    heads = q_in.shape[0] // tokens
    wide = wbuf.shape[4]
    depth = wbuf.shape[3]

    def block_of(other_z, other_y, other_k):
        in_z = zl + other_z * (1 - 2 * zl)
        in_y = y + other_y * (1 - 2 * y)
        in_k = k + other_k * (1 - 2 * k)
        return in_z * PLANE + in_y * 2 + in_k

    barrier = pltpu.get_barrier_semaphore()

    @pl.loop(1, n)
    def _(j):
        pl.semaphore_signal(barrier, inc=1, device_id=((c + j) % n, e), device_id_type=MESH)

    pl.semaphore_signal(barrier, inc=1, device_id=(c, 1 - e), device_id_type=MESH)
    mine = block_of(0, 0, 0)

    def own_load(f):
        return pltpu.make_async_copy(
            w_hbm.at[:, pl.ds(pl.multiple_of(e * half + f * wide, wide), wide)],
            wbuf.at[f, mine, e], local_sem.at[f],
        )

    load_q = pltpu.make_async_copy(q_hbm, q_in, local_sem.at[2])
    load_resid = pltpu.make_async_copy(resid_hbm, resid, local_sem.at[3])
    load_gu = pltpu.make_async_copy(gu_hbm, gu_raw, local_sem.at[4])
    load_down = pltpu.make_async_copy(down_hbm, down, local_sem.at[5])
    small = [
        pltpu.make_async_copy(source, held, local_sem.at[6 + i])
        for i, (source, held) in enumerate(
            (
                (key_hbm, key_ref), (value_hbm, value_ref), (gain_hbm, gain_ref),
                (ids_hbm, ids_ref), (gate_hbm, gate_ref),
            )
        )
    ]
    for copy in small:
        copy.start()
    load_w = pltpu.make_async_copy(w_hbm, w_held, local_sem.at[11])
    load_w.start()
    own_load(0).start()
    own_load(1).start()
    load_q.start()
    load_resid.start()
    load_gu.start()
    load_down.start()
    small[0].wait()
    small[1].wait()
    group = e * heads // (HQ // KVH)
    for part, source in enumerate((key_ref, value_ref)):
        picked = jnp.where(group == 0, source[:, 0, :].astype(F32), source[:, 1, :].astype(F32))
        kvbuf[c, part * tokens : (part + 1) * tokens, :] = picked.astype(BF16)
    pl.semaphore_wait(barrier, n)

    def kv_copy(block, slot, to):
        return pltpu.make_async_remote_copy(
            src_ref=kvbuf.at[block], dst_ref=kvbuf.at[block], send_sem=kv_send.at[slot],
            recv_sem=kv_recv.at[block], device_id=(to, e), device_id_type=MESH,
        )

    def w_copy(block, f, g, sem, to):
        return pltpu.make_async_remote_copy(
            src_ref=wbuf.at[f, block, g], dst_ref=wbuf.at[f, block, g], send_sem=sem,
            recv_sem=w_recv.at[block, f, g], device_id=(to, e), device_id_type=MESH,
        )

    def wait_block(block, f, g):
        w_copy(block, f, g, own_z.at[0, 0], sibling).wait_recv()

    def swap(f):
        return pltpu.make_async_remote_copy(
            src_ref=w_held.at[:, pl.ds(pl.multiple_of((1 - e) * half + f * wide, wide), wide)],
            dst_ref=wbuf.at[f, mine, e], send_sem=x_send.at[f], recv_sem=w_recv.at[mine, f, e],
            device_id=(c, 1 - e), device_id_type=MESH,
        )

    def group_of(s):
        return (e + s) % 2

    def send_own(f, s):
        g = group_of(s)
        w_copy(mine, f, g, own_z.at[f, g], z_peer).start()
        w_copy(mine, f, g, own_y.at[f, g], y_peer).start()
        w_copy(mine, f, g, w_sib.at[0, f, g], sibling).start()

    for step in range(1, N_Z):
        kv_copy(c, step - 1, ((z + step) % N_Z) * PLANE + plane).start()
    kv_copy(c, 3, y_peer).start()
    kv_copy(c, 7, sibling).start()
    load_w.wait()
    swap(0).start()
    swap(1).start()
    load_q.wait()
    rows32[...] = q_in[...].astype(F32)
    for step in range(1, N_Z):
        block = ((z + step) % N_Z) * PLANE + plane
        kv_copy(block, 0, sibling).wait_recv()
        kv_copy(block, 3 + step, y_peer).start()
        kv_copy(block, 7 + step, sibling).start()
    own_load(0).wait()
    send_own(0, 0)
    for step in range(N_Z):
        block = ((z + step) % N_Z) * PLANE + (1 - y) * 2 + k
        kv_copy(block, 0, sibling).wait_recv()
        kv_copy(block, 11 + step, sibling).start()
    wait_block(mine, 0, group_of(1))
    send_own(0, 1)
    own_load(1).wait()
    send_own(1, 0)
    wait_block(mine, 1, group_of(1))
    send_own(1, 1)
    depth_part = depth // 2
    row = lax.broadcasted_iota(jnp.int32, target.shape, 0)
    col = lax.broadcasted_iota(jnp.int32, target.shape, 1)
    target[...] = row - ((col % depth_part) // 8) * 128 - (col // depth_part) * 8 - col % 8
    for block_z in range(N_Z):
        for block_y in range(2):
            kv_copy(block_z * PLANE + block_y * 2 + 1 - k, 0, sibling).wait_recv()

    scale = math.log2(math.e) / math.sqrt(q_in.shape[1])
    n_keys = n * tokens

    def attend(pair):
        first = rows32[pl.ds(2 * pair, tokens, stride=heads), :]
        second = rows32[pl.ds(2 * pair + 1, tokens, stride=heads), :]
        both = jnp.concatenate([first, second], axis=0).astype(BF16)
        key_all = kvbuf[:, :tokens, :].reshape(n_keys, 128)
        value_all = kvbuf[:, tokens:, :].reshape(n_keys, 128)
        scores = lax.dot_general(
            both, key_all, (((1,), (1,)), ((), ())), preferred_element_type=F32
        )
        q_pos = c * tokens + lax.broadcasted_iota(jnp.int32, scores.shape, 0) % tokens
        k_pos = lax.broadcasted_iota(jnp.int32, scores.shape, 1)
        masked = jnp.where(k_pos <= q_pos, scores, masked_score)
        best = jnp.max(masked, axis=1, keepdims=True)
        prob = jnp.exp2((masked - best) * scale)
        total = jnp.sum(prob, axis=1, keepdims=True)
        part = jnp.dot(prob.astype(BF16), value_all, preferred_element_type=F32)
        done = (part / total).astype(BF16)
        turn = pair // (heads // 4)
        at = pair % (heads // 4) * 256
        ctx2d[turn, :, pl.ds(pl.multiple_of(at, 256), 128)] = done[:tokens]
        ctx2d[turn, :, pl.ds(pl.multiple_of(at + 128, 128), 128)] = done[tokens:]
        rows32[pl.ds(2 * pair, tokens, stride=heads), :] = done[:tokens].astype(F32)
        rows32[pl.ds(2 * pair + 1, tokens, stride=heads), :] = done[tokens:].astype(F32)

    def ctx_copy(slot, hh, src, dst, to):
        return pltpu.make_async_remote_copy(
            src_ref=src, dst_ref=dst, send_sem=c_send.at[slot, hh], recv_sem=c_recv.at[slot, hh],
            device_id=to, device_id_type=MESH,
        )

    def to_partner(hh):
        return ctx_copy(0, hh, ctxbuf.at[2, 0, hh], ctxbuf.at[1, e, hh], (partner, e))

    def over(slot, hh):
        return ctx_copy(1 + slot, hh, ctxbuf.at[slot, e, hh], ctxbuf.at[slot, e, hh], (c, 1 - e))

    def pass_on(hh):
        ctx_copy(0, hh, ctxbuf.at[1, e, hh], ctxbuf.at[1, e, hh], (partner, e)).wait_recv()
        over(1, hh).start()

    def pick_quad(hh, quad):
        pick = jnp.where(target[...] == 32 * quad, 1.0, 0.0).astype(BF16)
        return jnp.dot(ctx2d[hh], pick, preferred_element_type=F32).astype(BF16)

    @pl.loop(0, 2)
    def _(turn):
        @pl.loop(0, heads // 4)
        def _(step):
            attend(turn * (heads // 4) + step)

        @pl.loop(0, 2)
        def _(quad):
            ctxbuf[2, 0, turn, quad] = pick_quad(turn, (1 - zh) * 2 + quad)

        to_partner(turn).start()

        @pl.loop(0, 2)
        def _(quad):
            ctxbuf[0, e, turn, quad] = pick_quad(turn, zh * 2 + quad)

        over(0, turn).start()

        @pl.when(turn == 0)
        def _():
            @pl.loop(0, 2)
            def _(s):
                g = group_of(s)
                wait_block(block_of(1, 0, 0), 0, g)
                w_copy(block_of(1, 0, 0), 0, g, fwd_y.at[g], y_peer).start()
                w_copy(block_of(1, 0, 0), 0, g, w_sib.at[1, 0, g], sibling).start()
                wait_block(block_of(0, 1, 0), 0, g)
                w_copy(block_of(0, 1, 0), 0, g, w_sib.at[2, 0, g], sibling).start()

    pass_on(0)

    @pl.loop(0, 2)
    def _(s):
        g = group_of(s)
        wait_block(block_of(0, 1, 0), 1, g)
        w_copy(block_of(0, 1, 0), 1, g, fwd_z.at[g], z_peer).start()
        w_copy(block_of(0, 1, 0), 1, g, w_sib.at[2, 1, g], sibling).start()
        wait_block(block_of(1, 0, 0), 1, g)
        w_copy(block_of(1, 0, 0), 1, g, w_sib.at[1, 1, g], sibling).start()

    units = down.shape[0]
    unpack_rows = 128

    def unpack(first, count):
        @pl.loop(first, first + count)
        def _(i):
            at = pl.ds(pl.multiple_of(i * unpack_rows, unpack_rows), unpack_rows)
            gu[at, :units] = gu_raw[at, 0, :]
            gu[at, units:] = gu_raw[at, 1, :]

    n_unpack = half // unpack_rows
    load_gu.wait()
    unpack(0, n_unpack // 4)
    pass_on(1)

    def relay_far(f):
        @pl.loop(0, 2)
        def _(s):
            g = group_of(s)
            wait_block(block_of(1, 1, 0), f, g)
            w_copy(block_of(1, 1, 0), f, g, w_sib.at[3, f, g], sibling).start()

    relay_far(0)
    unpack(n_unpack // 4, n_unpack // 4)
    ctx_ref[...] = rows32[...].astype(BF16)
    acc[...] = jnp.zeros_like(acc)
    for hh in range(2):
        for slot in range(2):
            ctx_copy(
                1 + slot, hh, ctxbuf.at[slot, 1 - e, hh], ctxbuf.at[slot, 1 - e, hh], (c, 1 - e)
            ).wait_recv()

    def project(f):
        @pl.loop(0, 4)
        def _(i):
            other_z = i // 2
            g = group_of(i % 2)
            wait_block(block_of(other_z, 0, 1), f, g)
            wait_block(block_of(other_z, 1, 1), f, g)
            quad = zl + other_z * (1 - 2 * zl)
            for hh in range(2):
                weights = wbuf[
                    f, pl.ds(quad * PLANE, PLANE), pl.ds(g, 1), hh * depth_part : (hh + 1) * depth_part
                ].reshape(PLANE * depth_part, wide)
                lhs = jnp.concatenate([ctxbuf[0, g, hh, quad], ctxbuf[1, g, hh, quad]], axis=0)
                acc[f] += jnp.dot(lhs, weights, preferred_element_type=F32)

        part_out[f] = acc[f, tokens:, :].astype(BF16)
        pltpu.make_async_remote_copy(
            src_ref=part_out.at[f], dst_ref=part_in.at[f], send_sem=h_send.at[f],
            recv_sem=h_recv.at[f], device_id=(partner, e), device_id_type=MESH,
        ).start()

    def part_copy(f):
        return pltpu.make_async_remote_copy(
            src_ref=part_out.at[f], dst_ref=part_in.at[f], send_sem=h_send.at[f],
            recv_sem=h_recv.at[f], device_id=(partner, e), device_id_type=MESH,
        )

    project(0)
    relay_far(1)
    project(1)
    load_resid.wait()
    unpack(n_unpack // 2, n_unpack // 4)

    for copy in small[2:]:
        copy.wait()
    slot = lax.broadcasted_iota(jnp.int32, (rows, tokens), 0)
    named = jnp.zeros((rows, tokens), F32)
    share = jnp.zeros((rows, tokens), F32)
    gates = gate_ref[...]
    gates = gates / jnp.sum(gates, axis=0, keepdims=True)
    for column in range(TOPK):
        hit = ids_ref[column : column + 1, :] == slot // cap
        named = jnp.where(hit, 1.0, named)
        share = jnp.where(hit, gates[column : column + 1, :], share)
    before = jnp.where(
        lax.broadcasted_iota(jnp.int32, (tokens, tokens), 0)
        < lax.broadcasted_iota(jnp.int32, (tokens, tokens), 1),
        1.0,
        0.0,
    ).astype(BF16)
    rank = jnp.dot(named.astype(BF16), before, preferred_element_type=F32)
    chosen = jnp.logical_and(named > 0.5, rank == (slot % cap).astype(F32))
    pick_all = jnp.where(chosen, 1.0, 0.0).astype(BF16)
    mix = jnp.where(chosen, share, 0.0)
    mix_high = mix.astype(BF16)
    mixes[0] = mix_high
    mixes[1] = (mix - mix_high.astype(F32)).astype(BF16)

    own = jnp.zeros((tokens, 1), F32)
    for f in range(2):
        part_copy(f).wait_recv()
        at = pl.ds(f * wide, wide)
        state = resid[:, at].astype(F32) + (acc[f, :tokens, :] + part_in[f].astype(F32))
        hidden_buf[:, at] = state
        own += jnp.sum(state * state, axis=1, keepdims=True)
    squares[...] = jnp.broadcast_to(own, squares.shape)
    sq = pltpu.make_async_remote_copy(
        src_ref=squares, dst_ref=peer_squares, send_sem=sq_sem.at[0], recv_sem=sq_sem.at[1],
        device_id=(c, 1 - e), device_id_type=MESH,
    )
    sq.start()
    sq.wait()
    mean = (squares[:, :1] + peer_squares[:, :1]) / D
    normed = (hidden_buf[...] * lax.rsqrt(mean + epsilon) * gain_ref[...]).astype(BF16)
    normed_buf[...] = normed
    for j in range(blocks // 2):
        sent = jnp.dot(
            pick_all, normed_buf[:, j * 256 : (j + 1) * 256], preferred_element_type=F32
        )
        stage[pl.ds(2 * j, rows, stride=blocks), :] = sent[:, :128]
        stage[pl.ds(2 * j + 1, rows, stride=blocks), :] = sent[:, 128:]
    outbox[...] = stage[...].reshape(outbox.shape).astype(BF16)

    def a_copy(to):
        return pltpu.make_async_remote_copy(
            src_ref=outbox.at[to], dst_ref=inbox.at[c], send_sem=a_send.at[to],
            recv_sem=a_recv.at[c], device_id=(to, e), device_id_type=MESH,
        )

    def b_copy(to):
        return pltpu.make_async_remote_copy(
            src_ref=backbox.at[to], dst_ref=endbox.at[c], send_sem=b_send.at[to],
            recv_sem=b_recv.at[c], device_id=(to, e), device_id_type=MESH,
        )

    near_rows = rows // 2
    near_n = n // 2

    def half_of(t):
        return zh + t * (1 - 2 * zh)

    def from_half(box, sems, t):
        first = half_of(t) * near_n

        @pl.loop(0, near_n)
        def _(j):
            source = first + j

            @pl.when(source != c)
            def _():
                pltpu.make_async_remote_copy(
                    src_ref=box.at[source], dst_ref=box.at[source], send_sem=a_send.at[0],
                    recv_sem=sems.at[source], device_id=(source, e), device_id_type=MESH,
                ).wait_recv()

        part_stage = stage.at[pl.ds(0, near_rows * blocks)]
        part_stage[...] = box[pl.ds(first, near_n)].reshape(near_rows * blocks, 128).astype(F32)
        for j in range(blocks):
            two[t, :, j * 128 : (j + 1) * 128] = stage[
                pl.ds(j, near_rows, stride=blocks), :
            ].astype(BF16)

    def far_first(start):
        @pl.loop(0, near_n)
        def _(j):
            start((1 - zh) * near_n + (c + j) % near_n)

        @pl.loop(1, near_n)
        def _(j):
            start(zh * near_n + (c + j) % near_n)

    far_first(lambda to: a_copy(to).start())
    inbox[c] = outbox[c]
    unpack(3 * (n_unpack // 4), n_unpack // 4)
    width = parts.shape[4]

    def p_copy(t, m):
        return pltpu.make_async_remote_copy(
            src_ref=parts.at[t, m], dst_ref=peer_parts.at[t, m], send_sem=p_send.at[t, m],
            recv_sem=p_recv.at[t, m], device_id=(c, 1 - e), device_id_type=MESH,
        )

    n_parts = units // width

    @pl.loop(0, 2)
    def _(t):
        from_half(inbox, a_recv, t)
        for m in range(n_parts):
            for side in range(2):
                start = side * units + m * width
                parts[t, m, side] = jnp.dot(
                    two[t], gu[:, start : start + width], preferred_element_type=F32
                ).astype(BF16)
            p_copy(t, m).start()

    load_down.wait()

    @pl.loop(0, 2)
    def _(t):
        for m in range(n_parts):
            p_copy(t, m).wait_recv()
            gate = parts[t, m, 0].astype(F32) + peer_parts[t, m, 0].astype(F32)
            up = parts[t, m, 1].astype(F32) + peer_parts[t, m, 1].astype(F32)
            act[:, m * width : (m + 1) * width] = (gate / (1.0 + jnp.exp(-gate)) * up).astype(BF16)
        for j in range(blocks // 2):
            result = jnp.dot(
                act[...], down[:, j * 256 : (j + 1) * 256], preferred_element_type=F32
            )
            stage[pl.ds(2 * j, near_rows, stride=blocks), :] = result[:, :128]
            stage[pl.ds(2 * j + 1, near_rows, stride=blocks), :] = result[:, 128:]
        first = half_of(t) * near_n
        backbox[pl.ds(first, near_n)] = (
            stage[: near_rows * blocks, :].reshape((near_n,) + backbox.shape[1:]).astype(BF16)
        )

        @pl.loop(0, near_n)
        def _(j):
            to = first + (c + j) % near_n

            @pl.when(to != c)
            def _():
                b_copy(to).start()

    endbox[c] = backbox[c]

    @pl.loop(0, 2)
    def _(t):
        from_half(endbox, b_recv, t)
        at = pl.ds(pl.multiple_of(half_of(t) * near_rows, 16), near_rows)
        for part in range(2):
            hidden_buf[...] += lax.dot_general(
                mixes[part, at, :], two[t], (((0,), (0,)), ((), ())), preferred_element_type=F32
            )

    mixed_ref[...] = hidden_buf[...].astype(BF16)

    for slot_index in range(15):
        kv_copy(c, slot_index, sibling).wait_send()
    for f in range(2):
        swap(f).wait_send()
        part_copy(f).wait_send()
        to_partner(f).wait_send()
        over(0, f).wait_send()
        over(1, f).wait_send()

    @pl.loop(0, 2)
    def _(g):
        w_copy(mine, 0, g, fwd_y.at[g], sibling).wait_send()
        w_copy(mine, 0, g, fwd_z.at[g], sibling).wait_send()
        for f in range(2):
            w_copy(mine, f, g, own_z.at[f, g], sibling).wait_send()
            w_copy(mine, f, g, own_y.at[f, g], sibling).wait_send()
            for source in range(4):
                w_copy(mine, f, g, w_sib.at[source, f, g], sibling).wait_send()

    @pl.loop(1, n)
    def _(j):
        a_copy((c + j) % n).wait_send()
        b_copy((c + j) % n).wait_send()

    for t in range(2):
        for m in range(n_parts):
            p_copy(t, m).wait_send()


def fast_body(queries, keys, values, resid, gain, expert_ids, gate_scores, w_gate_up, w_down, w_out):
    tokens, heads, size = queries.shape
    n = lax.axis_size("ctx")
    half = resid.shape[1]
    wide = half // 2
    capacity = max(2, 5 * tokens * TOPK // (4 * EXPERTS))
    depth = heads * w_out.shape[1]
    units = w_down.shape[1]
    rows = n * capacity
    blocks = half // 128
    box = (n, capacity, blocks, 128)
    width = 256
    vmem = pl.BlockSpec(memory_space=pltpu.VMEM)
    hbm = pl.BlockSpec(memory_space=pltpu.HBM)
    dma = pltpu.SemaphoreType.DMA
    context, mixed = pl.pallas_call(
        layer_kernel,
        out_shape=(
            jax.ShapeDtypeStruct((tokens * heads, size), BF16),
            jax.ShapeDtypeStruct((tokens, half), BF16),
        ),
        in_specs=[hbm] * 10,
        out_specs=(vmem, vmem),
        scratch_shapes=[
            pltpu.VMEM(keys.shape, BF16), pltpu.VMEM(values.shape, BF16), pltpu.VMEM((1, half), F32),
            pltpu.VMEM((TOPK, tokens), jnp.int32), pltpu.VMEM((TOPK, tokens), F32),
            pltpu.VMEM((depth, 2 * half), BF16),
            pltpu.VMEM((tokens * heads, size), BF16),
            pltpu.VMEM((tokens, half), BF16),
            pltpu.VMEM((n, 2 * tokens, size), BF16),
            pltpu.VMEM((2, HALF_Z, 2, depth, wide), BF16),
            pltpu.VMEM((tokens * heads, size), F32),
            pltpu.VMEM((2, tokens, heads * size // 2), BF16),
            pltpu.VMEM((3, 2, 2, HALF_Z // PLANE, tokens, PLANE * depth // 2), BF16),
            pltpu.VMEM((heads * size // 2, PLANE * depth // 2), jnp.int32),
            pltpu.VMEM((2, 2 * tokens, wide), F32),
            pltpu.VMEM((2, tokens, wide), BF16),
            pltpu.VMEM((2, tokens, wide), BF16),
            pltpu.VMEM((half, 2, units), BF16),
            pltpu.VMEM((half, 2 * units), BF16),
            pltpu.VMEM((units, half), BF16),
            pltpu.VMEM((tokens, 128), F32),
            pltpu.VMEM((tokens, 128), F32),
            pltpu.VMEM((tokens, half), F32),
            pltpu.VMEM((rows * blocks, 128), F32),
            pltpu.VMEM((2, rows // 2, half), BF16),
            pltpu.VMEM(box, BF16), pltpu.VMEM(box, BF16), pltpu.VMEM(box, BF16), pltpu.VMEM(box, BF16),
            pltpu.VMEM((2, units // width, 2, rows // 2, width), BF16),
            pltpu.VMEM((2, units // width, 2, rows // 2, width), BF16),
            pltpu.VMEM((rows // 2, units), BF16),
            pltpu.VMEM((2, rows, tokens), BF16),
            pltpu.VMEM((tokens, half), BF16),
            dma((15,)), dma((n,)), dma((2, 2)), dma((2,)), dma((2, 2)), dma((2,)),
            dma((4, 2, 2)), dma((HALF_Z, 2, 2)), dma((2,)), dma((3, 2)), dma((3, 2)), dma((2,)), dma((2,)),
            dma((2,)), dma((2, units // width)), dma((2, units // width)),
            dma((n,)), dma((n,)), dma((n,)), dma((n,)), dma((12,)),
        ],
        compiler_params=pltpu.CompilerParams(
            collective_id=0, has_side_effects=True, vmem_limit_bytes=56 * 2**20
        ),
        name="layer",
    )(
        queries.reshape(tokens * heads, size), keys, values,
        w_out.reshape(depth, 2 * half), resid, gain.reshape(1, half), expert_ids.T, gate_scores.T,
        w_gate_up[0], w_down[0],
    )
    return (context.reshape(tokens, heads, size), mixed)


def solution(mesh):
    in_specs = (
        P("ctx", "exp", None),
        P("ctx", None, None),
        P("ctx", None, None),
        P("ctx", "exp"),
        P("exp"),
        P("ctx", None),
        P("ctx", None),
        P("ctx", "exp", None, None),
        P("ctx", None, "exp"),
        P("exp", "ctx", None),
    )
    out_specs = (P("ctx", "exp", None), P("ctx", "exp"))
    fits = mesh.shape["ctx"] == N_Z * PLANE and mesh.shape["exp"] == 2
    body = fast_body if fits else general_body
    return jax.shard_map(body, mesh=mesh, in_specs=in_specs, out_specs=out_specs, check_vma=False)
```
